256 devices in a mesh: pts: 32 (over x, z_hi, y), modes: 8 (over z_lo, core).
Axes of the slice: x: 4, y: 4, z: 8 (z_hi: 2, z_lo: 4; z = z_hi * 4 + z_lo), core: 2. Of those that a mesh axis runs over, the one named last changes fastest.
Arguments:
- density: bfloat16 [5120, 1024], P('pts'), may hold values from -6 to 6
- near_blocks: bfloat16 [27, 1024, 1024], P(None, 'modes'), may hold values from -0.09375 to 0.09375
- neighbour_atoms: int32 [5120, 27], P('pts'), may hold values from 0 to 5119, as said below
- neighbour_offsets: int32 [5120, 27], P('pts'), may hold values from 0 to 26, as said below
- neighbour_counts: int32 [5120], P('pts'), may hold values from 1 to 27, as said below
- centers: float32 [2, 5120], P(None, 'pts'), may hold values from -4 to 4
- local_points: float32 [2, 1024], replicated, may hold values from -0.5 to 0.5
- wavevectors: float32 [2, 16384], P(None, 'modes'), may hold values from -24 to 24
- spectral_weight: float32 [16384], P('modes'), may hold values from 0.1 to 4
Outputs:
- potential: float32 [5120, 1024], P('pts', 'modes')
The draws below stay inside these ranges and needn't reach their ends.
Inputs may be any that keep to these rules, and one draw needn't show every extreme that they name: `neighbour_atoms`: each neighbour of an atom lies, cyclically over the 5120 atoms, among the 160 atoms before the aligned block of 160 atoms holding it, that block, or the 160 atoms after it; in every block both ends of that range are named. `neighbour_offsets`: each row names every offset class once. `neighbour_counts`: every aligned block of 160 atoms holds an atom with 27 live slots and one with 1.
All inputs are finite; a program needn't handle non-finite values.
Results may differ from the reference program's by a relative error of at most 0.0012.
Values may be sent and summed in bfloat16 or wider, within the bound.
No kernel may reach another device: no remote copies, remote signals or barrier semaphores. Data moves between devices by JAX's collectives and lax.ppermute only.
A program may use at most 128 MiB of HBM per device.

```python
import math
import jax
import jax.numpy as jnp
from jax import lax

Q = 1024
NOFF = 27
ATOMS_DEV = 160
ATOMS = 5120
MODES = 16384
N_PTS = 32


def draw_neighbour_atoms(key, part):
    key = jax.random.fold_in(key, 11)
    relative = jax.random.randint(key, (ATOMS, NOFF), -ATOMS_DEV, 2 * ATOMS_DEV)
    rows = jnp.arange(ATOMS)
    local_row = rows % ATOMS_DEV
    first_col = (jnp.arange(NOFF) == 0)[None, :]
    relative = jnp.where((local_row == 0)[:, None] & first_col, -ATOMS_DEV, relative)
    relative = jnp.where((local_row == ATOMS_DEV - 1)[:, None] & first_col, 2 * ATOMS_DEV - 1, relative)
    return (((rows - local_row)[:, None] + relative) % ATOMS).astype(jnp.int32)


def one_permutation(row_key):
    return jax.random.permutation(row_key, NOFF)


def draw_neighbour_offsets(key, part):
    key = jax.random.fold_in(key, 23)
    row_keys = jax.random.split(key, ATOMS)
    return jax.vmap(one_permutation)(row_keys).astype(jnp.int32)


def draw_neighbour_counts(key, part):
    key = jax.random.fold_in(key, 37)
    counts = jax.random.randint(key, (ATOMS,), 1, NOFF + 1)
    local_row = jnp.arange(ATOMS) % ATOMS_DEV
    counts = jnp.where(local_row == 0, NOFF, counts)
    counts = jnp.where(local_row == 1, 1, counts)
    return counts.astype(jnp.int32)


def level_of(own_key, extent, cuts, smallest, top_value):
    gain, own = 1.0, jax.random.fold_in(own_key, 6)
    for position, parts in cuts:
        steps = jnp.exp(jax.random.uniform(jax.random.fold_in(own, position), (parts,), jnp.float32, smallest / len(cuts), top_value / len(cuts)))
        gain = gain * jnp.repeat(steps, extent[position] // parts).reshape([-1 if axis == position else 1 for axis in range(len(extent))])
    return gain


def noise(key, shape, width, reach, cuts=(), held_as=jnp.bfloat16):
    loudness = level_of(key, shape, cuts, -0.22, 0.18) if cuts else 1.0
    entries = jax.random.normal(key, shape, jnp.float32) * width * loudness
    return jnp.minimum(jnp.maximum(entries, -reach), reach).astype(held_as)


def setup_inputs(seed: int = 0) -> dict:
    key_list = jax.random.split(jax.random.key(seed), 10)
    density = noise(key_list[0], (ATOMS, Q), 1.0, 6.0, ((0, 32),))
    near_blocks = noise(key_list[1], (NOFF, Q, Q), (4 * Q) ** -0.5, 0.09375, ((1, 8),))
    neighbour_atoms = draw_neighbour_atoms(jax.random.fold_in(key_list[9], 71), 0)
    neighbour_offsets = draw_neighbour_offsets(jax.random.fold_in(key_list[9], 71), 0)
    neighbour_counts = draw_neighbour_counts(jax.random.fold_in(key_list[9], 71), 0)
    centers = jnp.clip(jax.random.uniform(key_list[5], (2, ATOMS), jnp.float32, -4.0, 4.0) * level_of(key_list[5], (2, ATOMS), ((1, 32),), -0.4, 0.0), -4.0, 4.0)
    local_points = jnp.clip(jax.random.uniform(key_list[6], (2, Q), jnp.float32, -0.5, 0.5), -0.5, 0.5)
    wavevectors = jnp.clip(jax.random.uniform(key_list[7], (2, MODES), jnp.float32, -24.0, 24.0) * level_of(key_list[7], (2, MODES), ((1, 8),), -0.4, 0.0), -24.0, 24.0)
    spectral_weight = jnp.clip(jnp.exp(math.log(4.0) - 3.6888794 * jax.random.uniform(key_list[8], (MODES,), jnp.float32) ** level_of(key_list[8], (MODES,), ((0, 8),), -0.2, 0.2)), 0.1, 4.0)
    return dict(density=density, near_blocks=near_blocks, neighbour_atoms=neighbour_atoms, neighbour_offsets=neighbour_offsets, neighbour_counts=neighbour_counts, centers=centers, local_points=local_points, wavevectors=wavevectors, spectral_weight=spectral_weight)


def phase_tables(point_pos, wave_pos):
    phase = point_pos[0][:, None] * wave_pos[0][None, :] + point_pos[1][:, None] * wave_pos[1][None, :]
    return jnp.concatenate([jnp.cos(phase), jnp.sin(phase)], axis=1).astype(jnp.bfloat16)

def center_phase(center_pos, wave_pos):
    return center_pos[0][:, None] * wave_pos[0][None, :] + center_pos[1][:, None] * wave_pos[1][None, :]

def spread_modes(weighted, cos_c, sin_c):
    real_part = weighted[0][None, :] * cos_c - weighted[1][None, :] * sin_c
    imag_part = weighted[0][None, :] * sin_c + weighted[1][None, :] * cos_c
    return jnp.concatenate([real_part, -imag_part], axis=1).astype(jnp.bfloat16)

def reference(density, near_blocks, neighbour_atoms, neighbour_offsets, neighbour_counts, centers, local_points, wavevectors, spectral_weight):
    tables = phase_tables(local_points, wavevectors)
    normalizer = 1.0 / math.sqrt(ATOMS * Q * MODES)
    dens_blocks = density.reshape(N_PTS, ATOMS_DEV, Q)
    cent_blocks = centers.reshape(2, N_PTS, ATOMS_DEV).transpose(1, 0, 2)

    def structure_step(running, block_item):
        block_density, block_centers = block_item
        form_factors = jnp.dot(block_density, tables, preferred_element_type=jnp.float32)
        angles = center_phase(block_centers, wavevectors)
        cos_c = jnp.cos(angles)
        sin_c = jnp.sin(angles)
        form_cos = form_factors[:, :MODES]
        form_sin = form_factors[:, MODES:]
        real_part = lax.optimization_barrier(jnp.sum(cos_c * form_cos - sin_c * form_sin, axis=0))
        imag_part = -lax.optimization_barrier(jnp.sum(sin_c * form_cos + cos_c * form_sin, axis=0))
        return (running + jnp.stack([real_part, imag_part]), None)
    structure, unused = lax.scan(structure_step, jnp.zeros((2, MODES), jnp.float32), (dens_blocks, cent_blocks))
    weighted = structure * (spectral_weight * normalizer)[None, :]
    padded = jnp.concatenate([density, jnp.zeros((1, Q), density.dtype)], axis=0)
    blocks_wide = near_blocks.astype(jnp.float32)
    slot_ids = jnp.arange(NOFF)
    class_ids = jnp.arange(NOFF)

    def block_out(block_item):
        block_density, block_centers, block_atoms, block_offsets, block_counts = block_item
        angles = center_phase(block_centers, wavevectors)
        spread = spread_modes(weighted, jnp.cos(angles), jnp.sin(angles))
        far_field = lax.dot_general(spread, tables, (((1,), (1,)), ((), ())), preferred_element_type=jnp.float32)
        live_slots = slot_ids[None, :] < block_counts[:, None]
        matches = (block_offsets[:, :, None] == class_ids[None, None, :]) & live_slots[:, :, None]
        picked = lax.optimization_barrier(jnp.sum(jnp.where(matches, block_atoms[:, :, None] + 1, 0), axis=1)) - 1
        picked = jnp.where(picked < 0, ATOMS, picked).astype(jnp.int32)
        gathered = jnp.take(padded, picked, axis=0).astype(jnp.float32)
        near_field = jnp.einsum('aoq,okq->ak', gathered, blocks_wide)
        return 0.5 * block_density.astype(jnp.float32) + near_field + far_field
    result = lax.map(block_out, (dens_blocks, cent_blocks, neighbour_atoms.reshape(N_PTS, ATOMS_DEV, NOFF), neighbour_offsets.reshape(N_PTS, ATOMS_DEV, NOFF), neighbour_counts.reshape(N_PTS, ATOMS_DEV)))
    return result.reshape(ATOMS, Q)
```

```python
import functools
import math

import jax
import jax.numpy as jnp
import numpy as np
from jax import lax
from jax.experimental import pallas as pl
from jax.experimental.pallas import tpu as pltpu
from jax.sharding import Mesh
from jax.sharding import PartitionSpec as P

BAND = 12.0
NODES = (
    0.04830766569, 0.1444719616, 0.2392873623, 0.3318686023, 0.4213512761, 0.5068999089, 0.5877157572, 0.6630442669, 0.7321821187, 0.794483796, 0.8493676137, 0.8963211558, 0.9349060759, 0.9647622556, 0.9856115115, 0.9972638618,
)
EVEN = (
    (0.264161544, 0.235683413, 0.1877892764, 0.1338856267, 0.08565638585, 0.04935936307, 0.02573553405, 0.01220462496, 0.005294905203, 0.00211445586, 0.0007820202318, 0.0002693802975, 8.679038294e-05, 2.6181341e-05, 7.331099629e-06, 1.708479253e-06),
    (0.1702613529, 0.08465650818, -0.04082940747, -0.1469360259, -0.1970030198, -0.1901061112, -0.1489564192, -0.09954602317, -0.05833865755, -0.03055765255, -0.01451635874, -0.006328267813, -0.002555179594, -0.0009609245647, -0.000333851875, -9.333966862e-05),
    (-0.1323973182, -0.02247601982, 0.1047497372, 0.1503633392, 0.08986991162, -0.02455938248, -0.1219371619, -0.1640572477, -0.1545048367, -0.1178161583, -0.07717100148, -0.0448976056, -0.02371842969, -0.01152257368, -0.005081924909, -0.001704677766),
    (-0.1038663831, 0.008772611212, 0.1112611228, 0.09900945939, -0.007887275225, -0.1049440761, -0.1157944762, -0.04697227583, 0.04443730952, 0.108316557, 0.1285622126, 0.1155652092, 0.08749662772, 0.05797221816, 0.03303595529, 0.01312861586),
    (-0.09524794649, 0.02681958951, 0.1142235556, 0.06137473355, -0.06159895528, -0.114537939, -0.05174444256, 0.05425346059, 0.1112188114, 0.08907465173, 0.01933187924, -0.05021028773, -0.08987667008, -0.09410761546, -0.0713193742, -0.03310624913),
    (0.1022051591, -0.05281704117, -0.1277713562, -0.0158252522, 0.116158395, 0.09060969529, -0.0463884297, -0.1239497875, -0.06822339825, 0.04641750905, 0.1115635062, 0.08861974282, 0.01440006111, -0.05133346873, -0.07076867034, -0.04114204128),
    (-0.1016349432, 0.081731359, 0.1180899649, -0.05213972209, -0.1310463958, 0.004828729775, 0.1285200703, 0.06026154641, -0.08513107212, -0.1134175056, -0.009982527353, 0.09053034847, 0.0894231339, 0.01200695961, -0.051135621, -0.04311496388),
    (-0.09691907606, 0.1086033655, 0.08463923718, -0.1138806091, -0.07938954229, 0.1091864505, 0.0866221684, -0.08980194788, -0.1037585862, 0.04854215716, 0.1134990489, 0.01271606801, -0.08781269714, -0.0609974537, 0.02562700126, 0.04324151356),
    (-0.08972912127, 0.1300425509, 0.03237330507, -0.1418919531, 0.02055363161, 0.132001602, -0.05367707241, -0.1161966312, 0.06348478865, 0.1052884638, -0.05273929295, -0.09804759123, 0.02676341234, 0.0825150306, 0.001318540609, -0.04206423821),
    (-0.0807528844, 0.1433856071, -0.02927536699, -0.1203274859, 0.113532529, 0.04297640002, -0.1359071454, 0.03217281435, 0.1131044363, -0.07497313561, -0.07767707065, 0.08565207726, 0.04832778656, -0.07373331536, -0.0262794175, 0.03977430954),
)
ODD = (
    (-0.06039643671, -0.1619285065, -0.2157655924, -0.2164663713, -0.179285157, -0.1273735765, -0.07932182359, -0.04395383706, -0.0219317145, -0.009956138688, -0.004149848215, -0.001600910605, -0.0005751981407, -0.0001930716936, -6.006259695e-05, -1.532579998e-05),
    (0.06770405989, 0.1570721263, 0.1434280287, 0.04295191184, -0.07879962265, -0.1610074452, -0.1820744199, -0.1564850599, -0.1117106857, -0.06911197019, -0.03803899989, -0.018976138, -0.008700246907, -0.003698004317, -0.001443221181, -0.0004421770918),
    (-0.06672308627, -0.1353009509, -0.07559650806, 0.05145652305, 0.1328476776, 0.1110923906, 0.01620622731, -0.08318512773, -0.1393111579, -0.1451173835, -0.1191406959, -0.08344766078, -0.05189716398, -0.02921471538, -0.01463357191, -0.005358686102),
    (-0.06188570509, -0.1120544487, -0.03164468805, 0.08318098917, 0.1076065769, 0.02554639647, -0.07633334629, -0.1130798134, -0.07076087078, 0.008202589998, 0.07547632887, 0.1077871043, 0.1068753005, 0.08546497618, 0.0555295236, 0.02380489812),
    (0.07294621453, 0.1170272587, 0.0005822684711, -0.1151664239, -0.08239886349, 0.04808258285, 0.1205972232, 0.06802484515, -0.04264531193, -0.1109041826, -0.09690224579, -0.0289313287, 0.0417153054, 0.07952536804, 0.07530043037, 0.03856509779),
    (0.08652145766, 0.1159240548, -0.04433348034, -0.1318825677, -0.0146605442, 0.1210590442, 0.0842447592, -0.05956973628, -0.1239316034, -0.0494564638, 0.06563154857, 0.1089604688, 0.06071412772, -0.01917666675, -0.06207287706, -0.04244003862),
    (0.09796928773, 0.1014768063, -0.091850156, -0.1080980874, 0.07605361357, 0.1198048209, -0.04229231028, -0.1286411677, -0.01461539232, 0.1112662457, 0.07892093947, -0.04457606115, -0.09810478366, -0.03937820657, 0.03879814661, 0.04335854939),
    (0.1083285032, 0.07708721735, -0.1285703026, -0.0450395491, 0.1354076647, 0.02413735124, -0.1328629117, -0.02187888439, 0.1235455303, 0.03873152733, -0.1025408614, -0.0647085451, 0.06221363399, 0.07559191195, -0.01210690766, -0.04280157103),
    (0.1177268554, 0.04504968521, -0.1441555522, 0.03839419971, 0.1212170689, -0.09675550887, -0.07572314606, 0.120135559, 0.03631601591, -0.1190390193, -0.01579049946, 0.1052262271, 0.01219152635, -0.08172301286, -0.01423910674, 0.04104943366),
    (0.126120285, 0.007979130802, -0.1328480522, 0.1116338241, 0.03421605314, -0.1374354291, 0.07279981158, 0.07996744654, -0.1205095327, -0.004441967651, 0.111290914, -0.04516234118, -0.07618300914, 0.05955705328, 0.03710370067, -0.03825468552),
)
EVEN_GAIN = (
    0.7236012542, -0.7236000597, 0.7230899637, -0.6794753044, 0.309908605, -0.04203461377, 0.003110230195, -0.0001597812355, 6.121678833e-06, -1.82449892e-07,
)
ODD_GAIN = (
    0.7236012257, -0.7235710907, 0.7176666509, -0.5402161025, 0.127514432, -0.01205222733, 0.0007337517912, -3.234542573e-05, 1.088270167e-06, -2.894614862e-08,
)
RANK = 10
TURN = 1.0 / (2.0 * math.pi)
SIN_COEFS = (
    6.283182818550517, -41.3414213986335, 81.59618387150637,
    -76.58010050946145, 41.20539479011024, -12.271262230884131,
)
COS_COEFS = (
    0.9999999891722597, -19.739204532088525, 64.93911898360994, -85.45016554540021,
    60.167831693053074, -25.96831316496443, 6.52961023180932,
)
MODE_TILE = 512
CLASS_TILE = 9
VMEM_LIMIT = 48 * 1024 * 1024
NT = (((1,), (1,)), ((), ()))
NN = (((1,), (0,)), ((), ()))


def horner(coefs, square):
    total = jnp.full_like(square, coefs[-1])
    for coef in coefs[-2::-1]:
        total = total * square + coef
    return total


def cos_sin(turns):
    rest = turns - jnp.round(turns)
    square = rest * rest
    return horner(COS_COEFS, square), rest * horner(SIN_COEFS, square)


def dot(a, b, dims=NN):
    return lax.dot_general(a, b, dims, preferred_element_type=jnp.float32)


def dot_wide(a, b):
    return lax.dot_general(
        a, b, NN, precision=lax.Precision.HIGHEST, preferred_element_type=jnp.float32
    )


def split(value):
    high = value.astype(jnp.bfloat16)
    return high, (value - high.astype(jnp.float32)).astype(jnp.bfloat16)


def dot_split(a, b, dims=NN):
    return dot(a[0], b[0], dims) + (dot(a[0], b[1], dims) + dot(a[1], b[0], dims))


def outer_rows(left, right):
    rows = [left[:8] * right[i : i + 1] for i in range(RANK)]
    rows += [left[i : i + 1] * right[:8] for i in range(8, RANK)]
    return jnp.concatenate(rows, axis=0)


def factors(first, second, nodes, even, odd):
    width = first.shape[1]
    cos_part, sin_part = cos_sin(nodes * jnp.concatenate([first, second], axis=1))
    evens = dot_wide(even, cos_part)
    odds = dot_wide(odd, sin_part)
    return evens[:, :width], odds[:, :width], evens[:, width:], odds[:, width:]


def as_column(row):
    count = row.shape[1]
    here = lax.broadcasted_iota(jnp.int32, (count, count), 0)
    there = lax.broadcasted_iota(jnp.int32, (count, count), 1)
    return jnp.sum(jnp.where(here == there, row, 0.0), axis=1, keepdims=True)


def structure_kernel(
    density, centers, points, waves, nodes, even_x, odd_x, even_k, odd_k,
    partial, cos_out, sin_out, wave_c_high, wave_c_low, wave_s_high, wave_s_low,
    point_c_high, point_c_low, point_s_high, point_s_low,
    form_c_high, form_c_low, form_s_high, form_s_low, center_x, center_y,
):
    @pl.when(pl.program_id(0) == 0)
    def prepare():
        evx, odx, evy, ody = factors(
            points[0:1, :] * (2.0 * BAND * TURN), points[1:2, :] * (2.0 * BAND * TURN),
            nodes[...], even_x[...], odd_x[...],
        )
        cos_rows = split(jnp.concatenate([outer_rows(evx, evy), -outer_rows(odx, ody)], axis=0))
        sin_rows = split(jnp.concatenate([outer_rows(odx, evy), outer_rows(evx, ody)], axis=0))
        point_c_high[...], point_c_low[...] = cos_rows
        point_s_high[...], point_s_low[...] = sin_rows
        dens = density[...]
        form_c_high[...], form_c_low[...] = split(
            dot(dens, cos_rows[0], NT) + dot(dens, cos_rows[1], NT)
        )
        form_s_high[...], form_s_low[...] = split(
            dot(dens, sin_rows[0], NT) + dot(dens, sin_rows[1], NT)
        )
        center_x[...] = as_column(centers[0:1, :])
        center_y[...] = as_column(centers[1:2, :])

    kx = waves[0:1, :] * TURN
    ky = waves[1:2, :] * TURN
    evx, odx, evy, ody = factors(
        kx * (BAND / 24.0), ky * (BAND / 24.0), nodes[...], even_k[...], odd_k[...]
    )
    cos_rows = split(jnp.concatenate([outer_rows(evx, evy), outer_rows(odx, ody)], axis=0))
    sin_rows = split(jnp.concatenate([outer_rows(odx, evy), outer_rows(evx, ody)], axis=0))
    wave_c_high[...], wave_c_low[...] = cos_rows
    wave_s_high[...], wave_s_low[...] = sin_rows
    cos_c, sin_c = cos_sin(center_x[...] * kx + center_y[...] * ky)
    cos_out[...] = cos_c
    sin_out[...] = sin_c
    form_cos = dot_split((form_c_high[...], form_c_low[...]), cos_rows)
    form_sin = dot_split((form_s_high[...], form_s_low[...]), sin_rows)
    partial[0:1, :] = jnp.sum(cos_c * form_cos - sin_c * form_sin, axis=0, keepdims=True)
    partial[1:2, :] = -jnp.sum(sin_c * form_cos + cos_c * form_sin, axis=0, keepdims=True)


def partial_structure(density, centers, points, waves):
    atoms, count = density.shape
    modes = waves.shape[1]
    rows = 2 * (8 * RANK + 8 * (RANK - 8))
    tile = min(MODE_TILE, modes)
    nodes = np.array(NODES, np.float32)[:, None]
    pad = ((0, 16 - RANK), (0, 0))
    even = np.pad(np.array(EVEN), pad).astype(np.float32)
    odd = np.pad(np.array(ODD), pad).astype(np.float32)
    even_k = np.pad(np.array(EVEN) / np.array(EVEN_GAIN)[:, None], pad).astype(np.float32)
    odd_k = np.pad(np.array(ODD) / np.array(ODD_GAIN)[:, None], pad).astype(np.float32)
    whole = lambda shape: pl.BlockSpec(shape, lambda i: (0, 0))
    tiled = lambda height: pl.BlockSpec((height, tile), lambda i: (0, i))
    bf16 = jnp.bfloat16
    out = lambda shape, kind: jax.ShapeDtypeStruct(shape, kind)
    return pl.pallas_call(
        structure_kernel,
        grid=(modes // tile,),
        in_specs=[
            whole((atoms, count)), whole((2, atoms)), whole((2, count)), tiled(2),
            whole((16, 1)), whole((16, 16)), whole((16, 16)), whole((16, 16)), whole((16, 16)),
        ],
        out_specs=[tiled(2), tiled(atoms), tiled(atoms)] + [tiled(rows)] * 4
        + [whole((rows, count))] * 4,
        out_shape=[out((2, modes), jnp.float32)] + [out((atoms, modes), jnp.float32)] * 2
        + [out((rows, modes), bf16)] * 4 + [out((rows, count), bf16)] * 4,
        scratch_shapes=[pltpu.VMEM((atoms, rows), bf16)] * 4
        + [pltpu.VMEM((atoms, 1), jnp.float32)] * 2,
        compiler_params=pltpu.CompilerParams(vmem_limit_bytes=VMEM_LIMIT),
        cost_estimate=pl.CostEstimate(
            flops=2 * atoms * rows * (count * 4 + modes * 6),
            bytes_accessed=8 * atoms * modes, transcendentals=0,
        ),
    )(density, centers, points, waves, nodes, even, odd, even_k, odd_k)


def far_kernel(
    place, first, second, weight, cos_c, sin_c,
    wave_c_high, wave_c_low, wave_s_high, wave_s_low,
    point_c_high, point_c_low, point_s_high, point_s_low,
    keep, send, held_c, held_s, field,
):
    step = pl.program_id(0)
    scaled = weight[...]
    real = (first[0:1, :] + second[0:1, :]) * scaled
    imag = (first[1:2, :] + second[1:2, :]) * scaled
    cosine, sine = cos_c[...], sin_c[...]
    spread_c = split(real * cosine - imag * sine)
    spread_s = split(-(real * sine + imag * cosine))
    part_c = dot_split(spread_c, (wave_c_high[...], wave_c_low[...]), NT)
    part_s = dot_split(spread_s, (wave_s_high[...], wave_s_low[...]), NT)

    @pl.when(step == 0)
    def begin():
        held_c[...] = part_c
        held_s[...] = part_s

    @pl.when(step > 0)
    def add():
        held_c[...] += part_c
        held_s[...] += part_s

    @pl.when(step == pl.num_programs(0) - 1)
    def finish():
        field[...] = dot_split(
            split(held_c[...]), (point_c_high[...], point_c_low[...])
        ) + dot_split(split(held_s[...]), (point_s_high[...], point_s_low[...]))
        chip, core = place[0], place[1]
        chips, _, width = keep.shape
        for ahead in range(chips):
            other = lax.rem(chip + ahead, chips)
            mine = pl.multiple_of((2 * other + core) * width, width)
            theirs = pl.multiple_of((2 * other + 1 - core) * width, width)
            keep[ahead] = field[:, pl.ds(mine, width)]
            send[ahead] = field[:, pl.ds(theirs, width)]


def far_partial(place, first, second, weight, cos_c, sin_c, waves, points, chips):
    atoms, modes = cos_c.shape
    rows, count = points[0].shape
    tile = min(MODE_TILE, modes)
    width = count // (2 * chips)
    whole = lambda shape: pl.BlockSpec(shape, lambda i, s: (0, 0))
    tiled = lambda height: pl.BlockSpec((height, tile), lambda i, s: (0, i))
    blocks = pl.BlockSpec((chips, atoms, width), lambda i, s: (0, 0, 0))
    return pl.pallas_call(
        far_kernel,
        grid_spec=pltpu.PrefetchScalarGridSpec(
            num_scalar_prefetch=1,
            grid=(modes // tile,),
            in_specs=[tiled(2), tiled(2), tiled(1), tiled(atoms), tiled(atoms)]
            + [tiled(rows)] * 4 + [whole((rows, count))] * 4,
            out_specs=[blocks, blocks],
            scratch_shapes=[pltpu.VMEM((atoms, rows), jnp.float32)] * 2
            + [pltpu.VMEM((atoms, count), jnp.float32)],
        ),
        out_shape=[jax.ShapeDtypeStruct((chips, atoms, width), jnp.float32)] * 2,
        compiler_params=pltpu.CompilerParams(vmem_limit_bytes=VMEM_LIMIT),
        cost_estimate=pl.CostEstimate(
            flops=2 * atoms * rows * 6 * (count + modes),
            bytes_accessed=8 * atoms * modes, transcendentals=0,
        ),
    )(place, first, second, weight, cos_c, sin_c, *waves, *points)


def near_kernel(bases, offsets, places, near, *rest):
    sources, (out, total) = rest[:-2], rest[-2:]
    step = pl.program_id(0)
    classes, width, count = near.shape
    dens = [source[...] for source in sources]
    if len(dens) > 1:
        dens = jnp.concatenate(dens, axis=0)
    else:
        dens = dens[0]
    made = dot(dens, near[...].reshape(classes * width, count), NT)
    atoms = offsets.shape[0]
    here = dens.shape[0] // len(sources)
    column = lax.broadcasted_iota(jnp.int32, (atoms, dens.shape[0]), 1)
    base = jnp.where(column < here, bases[0], bases[len(sources) - 1] - here * (len(sources) - 1))
    target = (column + base).astype(jnp.float32)
    of_slot = offsets[...]
    place_of_slot = places[...]
    result = jnp.zeros((atoms, 2 * width), jnp.float32)
    for one in range(classes):
        hit = of_slot == step * classes + one
        found = jnp.sum(jnp.where(hit, place_of_slot, 0.0), axis=1, keepdims=True)
        chosen = jnp.where(found == target, 1.0, 0.0).astype(jnp.bfloat16)
        value = jnp.concatenate(split(made[:, one * width : (one + 1) * width]), axis=1)
        result = result + dot(chosen, value)
    result = result[:, :width] + result[:, width:]

    @pl.when(step == 0)
    def begin():
        total[...] = result

    @pl.when(step > 0)
    def add():
        total[...] += result

    @pl.when(step == pl.num_programs(0) - 1)
    def finish():
        out[...] = total[...]


def near_part(bases, offsets, places, near, sources):
    atoms, slots = offsets.shape
    classes, width, count = near.shape
    group = CLASS_TILE if classes % CLASS_TILE == 0 else 1
    whole = lambda shape: pl.BlockSpec(shape, lambda i, s: (0, 0))
    rows = atoms * len(sources)
    return pl.pallas_call(
        near_kernel,
        grid_spec=pltpu.PrefetchScalarGridSpec(
            num_scalar_prefetch=1,
            grid=(classes // group,),
            in_specs=[
                whole((atoms, slots)), whole((atoms, slots)),
                pl.BlockSpec((group, width, count), lambda i, s: (i, 0, 0)),
            ] + [whole((atoms, count))] * len(sources),
            out_specs=whole((atoms, width)),
            scratch_shapes=[pltpu.VMEM((atoms, width), jnp.float32)],
        ),
        out_shape=jax.ShapeDtypeStruct((atoms, width), jnp.float32),
        compiler_params=pltpu.CompilerParams(vmem_limit_bytes=VMEM_LIMIT),
        cost_estimate=pl.CostEstimate(
            flops=2 * rows * classes * width * (count + 2 * atoms),
            bytes_accessed=2 * classes * width * count, transcendentals=0,
        ),
    )(bases, offsets, places, near, *sources)


def fold_kernel(keep, taken, *outs):
    for ahead, out in enumerate(outs):
        out[...] = keep[ahead] + taken[ahead]


def fold(keep, taken):
    chips, atoms, width = keep.shape
    return pl.pallas_call(
        fold_kernel,
        out_shape=[jax.ShapeDtypeStruct((atoms, width), jnp.float32)] * chips,
        compiler_params=pltpu.CompilerParams(vmem_limit_bytes=VMEM_LIMIT),
    )(keep, taken)


def shifted(value, axis, by):
    count = lax.axis_size(axis)
    return lax.ppermute(value, axis, [(i, (i + by) % count) for i in range(count)])


def sum_over(value, axis):
    count = lax.axis_size(axis)
    return value + sum(shifted(value, axis, by) for by in range(1, count))


BLOCK_AXES = ("x", "z_hi", "y")


def shards(
    density, near_blocks, neighbour_atoms, neighbour_offsets, neighbour_counts,
    centers, local_points, wavevectors, spectral_weight,
):
    atoms, points = density.shape
    blocks = lax.axis_size(BLOCK_AXES)
    modes = wavevectors.shape[1]
    chips, cores = lax.axis_size("z_lo"), lax.axis_size("core")
    core, chip, block = lax.axis_index("core"), lax.axis_index("z_lo"), lax.axis_index(BLOCK_AXES)
    width = points // (chips * cores)
    normalizer = 1.0 / math.sqrt(atoms * blocks * points * modes * chips * cores)

    halo_route = []
    for source in range(blocks):
        halo_route.append((2 * source, 2 * ((source + 1) % blocks)))
        halo_route.append((2 * source + 1, 2 * ((source - 1) % blocks) + 1))
    halo = lax.ppermute(density, BLOCK_AXES + ("core",), halo_route)

    partial, cos_c, sin_c, *tables = partial_structure(density, centers, local_points, wavevectors)

    total_atoms = atoms * blocks
    places = (neighbour_atoms - (block - 1) * atoms + total_atoms) % total_atoms
    live = jnp.arange(neighbour_atoms.shape[1])[None, :] < neighbour_counts[:, None]
    places = jnp.where(live, places, -1).astype(jnp.float32)
    places = places + 1.0
    one = jnp.ones((1,), jnp.int32)
    near_own = near_part(one * (atoms + 1), neighbour_offsets, places, near_blocks, [density])

    structure = sum_over(partial, "y")
    structure = sum_over(structure, "x")
    other_half = shifted(structure, "z_hi", 1)

    halo_other = lax.ppermute(halo, "core", [(0, 1), (1, 0)])
    low, high = 1, 2 * atoms + 1
    bases = jnp.stack([jnp.where(core == 0, low, high), jnp.where(core == 0, high, low)])
    near_halo = near_part(
        bases.astype(jnp.int32), neighbour_offsets, places, near_blocks, [halo, halo_other]
    )

    weight = (spectral_weight * normalizer)[None, :]
    place = jnp.stack([chip, core]).astype(jnp.int32)
    keep, send = far_partial(
        place, structure, other_half, weight, cos_c, sin_c, tables[:4], tables[4:], chips
    )
    taken = lax.ppermute(send, "core", [(0, 1), (1, 0)])
    pieces = fold(keep, taken)
    far_field = pieces[0]
    for by in range(1, chips):
        far_field = far_field + shifted(pieces[by], "z_lo", by)
    member = chip * cores + core
    own = lax.dynamic_slice_in_dim(density, member * width, width, 1).astype(jnp.float32)
    return 0.5 * own + near_own + near_halo + far_field


def solution(mesh):
    fine = Mesh(
        mesh.devices.reshape(4, 2, 4, 4, 2), ("x", "z_hi", "y", "z_lo", "core")
    )
    modes = ("z_lo", "core")
    placed = (
        P(BLOCK_AXES, None), P(None, modes, None), P(BLOCK_AXES, None), P(BLOCK_AXES, None),
        P(BLOCK_AXES), P(None, BLOCK_AXES), P(), P(None, modes), P(modes),
    )
    return jax.shard_map(
        shards, mesh=fine, in_specs=placed, out_specs=P(BLOCK_AXES, modes), check_vma=False
    )
```

```python
import functools
import math

import jax
import jax.numpy as jnp
import numpy as np
from jax import lax
from jax.experimental import pallas as pl
from jax.experimental.pallas import tpu as pltpu
from jax.sharding import Mesh
from jax.sharding import PartitionSpec as P

BAND = 12.0
NODES = (
    0.04830766569, 0.1444719616, 0.2392873623, 0.3318686023, 0.4213512761, 0.5068999089, 0.5877157572, 0.6630442669, 0.7321821187, 0.794483796, 0.8493676137, 0.8963211558, 0.9349060759, 0.9647622556, 0.9856115115, 0.9972638618,
)
EVEN = (
    (0.264161544, 0.235683413, 0.1877892764, 0.1338856267, 0.08565638585, 0.04935936307, 0.02573553405, 0.01220462496, 0.005294905203, 0.00211445586, 0.0007820202318, 0.0002693802975, 8.679038294e-05, 2.6181341e-05, 7.331099629e-06, 1.708479253e-06),
    (0.1702613529, 0.08465650818, -0.04082940747, -0.1469360259, -0.1970030198, -0.1901061112, -0.1489564192, -0.09954602317, -0.05833865755, -0.03055765255, -0.01451635874, -0.006328267813, -0.002555179594, -0.0009609245647, -0.000333851875, -9.333966862e-05),
    (-0.1323973182, -0.02247601982, 0.1047497372, 0.1503633392, 0.08986991162, -0.02455938248, -0.1219371619, -0.1640572477, -0.1545048367, -0.1178161583, -0.07717100148, -0.0448976056, -0.02371842969, -0.01152257368, -0.005081924909, -0.001704677766),
    (-0.1038663831, 0.008772611212, 0.1112611228, 0.09900945939, -0.007887275225, -0.1049440761, -0.1157944762, -0.04697227583, 0.04443730952, 0.108316557, 0.1285622126, 0.1155652092, 0.08749662772, 0.05797221816, 0.03303595529, 0.01312861586),
    (-0.09524794649, 0.02681958951, 0.1142235556, 0.06137473355, -0.06159895528, -0.114537939, -0.05174444256, 0.05425346059, 0.1112188114, 0.08907465173, 0.01933187924, -0.05021028773, -0.08987667008, -0.09410761546, -0.0713193742, -0.03310624913),
    (0.1022051591, -0.05281704117, -0.1277713562, -0.0158252522, 0.116158395, 0.09060969529, -0.0463884297, -0.1239497875, -0.06822339825, 0.04641750905, 0.1115635062, 0.08861974282, 0.01440006111, -0.05133346873, -0.07076867034, -0.04114204128),
    (-0.1016349432, 0.081731359, 0.1180899649, -0.05213972209, -0.1310463958, 0.004828729775, 0.1285200703, 0.06026154641, -0.08513107212, -0.1134175056, -0.009982527353, 0.09053034847, 0.0894231339, 0.01200695961, -0.051135621, -0.04311496388),
    (-0.09691907606, 0.1086033655, 0.08463923718, -0.1138806091, -0.07938954229, 0.1091864505, 0.0866221684, -0.08980194788, -0.1037585862, 0.04854215716, 0.1134990489, 0.01271606801, -0.08781269714, -0.0609974537, 0.02562700126, 0.04324151356),
    (-0.08972912127, 0.1300425509, 0.03237330507, -0.1418919531, 0.02055363161, 0.132001602, -0.05367707241, -0.1161966312, 0.06348478865, 0.1052884638, -0.05273929295, -0.09804759123, 0.02676341234, 0.0825150306, 0.001318540609, -0.04206423821),
    (-0.0807528844, 0.1433856071, -0.02927536699, -0.1203274859, 0.113532529, 0.04297640002, -0.1359071454, 0.03217281435, 0.1131044363, -0.07497313561, -0.07767707065, 0.08565207726, 0.04832778656, -0.07373331536, -0.0262794175, 0.03977430954),
)
ODD = (
    (-0.06039643671, -0.1619285065, -0.2157655924, -0.2164663713, -0.179285157, -0.1273735765, -0.07932182359, -0.04395383706, -0.0219317145, -0.009956138688, -0.004149848215, -0.001600910605, -0.0005751981407, -0.0001930716936, -6.006259695e-05, -1.532579998e-05),
    (0.06770405989, 0.1570721263, 0.1434280287, 0.04295191184, -0.07879962265, -0.1610074452, -0.1820744199, -0.1564850599, -0.1117106857, -0.06911197019, -0.03803899989, -0.018976138, -0.008700246907, -0.003698004317, -0.001443221181, -0.0004421770918),
    (-0.06672308627, -0.1353009509, -0.07559650806, 0.05145652305, 0.1328476776, 0.1110923906, 0.01620622731, -0.08318512773, -0.1393111579, -0.1451173835, -0.1191406959, -0.08344766078, -0.05189716398, -0.02921471538, -0.01463357191, -0.005358686102),
    (-0.06188570509, -0.1120544487, -0.03164468805, 0.08318098917, 0.1076065769, 0.02554639647, -0.07633334629, -0.1130798134, -0.07076087078, 0.008202589998, 0.07547632887, 0.1077871043, 0.1068753005, 0.08546497618, 0.0555295236, 0.02380489812),
    (0.07294621453, 0.1170272587, 0.0005822684711, -0.1151664239, -0.08239886349, 0.04808258285, 0.1205972232, 0.06802484515, -0.04264531193, -0.1109041826, -0.09690224579, -0.0289313287, 0.0417153054, 0.07952536804, 0.07530043037, 0.03856509779),
    (0.08652145766, 0.1159240548, -0.04433348034, -0.1318825677, -0.0146605442, 0.1210590442, 0.0842447592, -0.05956973628, -0.1239316034, -0.0494564638, 0.06563154857, 0.1089604688, 0.06071412772, -0.01917666675, -0.06207287706, -0.04244003862),
    (0.09796928773, 0.1014768063, -0.091850156, -0.1080980874, 0.07605361357, 0.1198048209, -0.04229231028, -0.1286411677, -0.01461539232, 0.1112662457, 0.07892093947, -0.04457606115, -0.09810478366, -0.03937820657, 0.03879814661, 0.04335854939),
    (0.1083285032, 0.07708721735, -0.1285703026, -0.0450395491, 0.1354076647, 0.02413735124, -0.1328629117, -0.02187888439, 0.1235455303, 0.03873152733, -0.1025408614, -0.0647085451, 0.06221363399, 0.07559191195, -0.01210690766, -0.04280157103),
    (0.1177268554, 0.04504968521, -0.1441555522, 0.03839419971, 0.1212170689, -0.09675550887, -0.07572314606, 0.120135559, 0.03631601591, -0.1190390193, -0.01579049946, 0.1052262271, 0.01219152635, -0.08172301286, -0.01423910674, 0.04104943366),
    (0.126120285, 0.007979130802, -0.1328480522, 0.1116338241, 0.03421605314, -0.1374354291, 0.07279981158, 0.07996744654, -0.1205095327, -0.004441967651, 0.111290914, -0.04516234118, -0.07618300914, 0.05955705328, 0.03710370067, -0.03825468552),
)
EVEN_GAIN = (
    0.7236012542, -0.7236000597, 0.7230899637, -0.6794753044, 0.309908605, -0.04203461377, 0.003110230195, -0.0001597812355, 6.121678833e-06, -1.82449892e-07,
)
ODD_GAIN = (
    0.7236012257, -0.7235710907, 0.7176666509, -0.5402161025, 0.127514432, -0.01205222733, 0.0007337517912, -3.234542573e-05, 1.088270167e-06, -2.894614862e-08,
)
RANK = 10
TURN = 1.0 / (2.0 * math.pi)
SIN_COEFS = (
    6.283182818550517, -41.3414213986335, 81.59618387150637,
    -76.58010050946145, 41.20539479011024, -12.271262230884131,
)
COS_COEFS = (
    0.9999999891722597, -19.739204532088525, 64.93911898360994, -85.45016554540021,
    60.167831693053074, -25.96831316496443, 6.52961023180932,
)
MODE_TILE = 512
CLASS_TILE = 9
NT = (((1,), (1,)), ((), ()))
NN = (((1,), (0,)), ((), ()))
BLOCK_AXES = ("x", "z_hi", "y")
MIB = 1024 * 1024


def horner(coefs, square):
    total = jnp.full_like(square, coefs[-1])
    for coef in coefs[-2::-1]:
        total = total * square + coef
    return total


def cos_sin(turns):
    rest = turns - jnp.round(turns)
    square = rest * rest
    return horner(COS_COEFS, square), rest * horner(SIN_COEFS, square)


def dot(a, b, dims=NN):
    return lax.dot_general(a, b, dims, preferred_element_type=jnp.float32)


def split(value):
    high = value.astype(jnp.bfloat16)
    return high, (value - high.astype(jnp.float32)).astype(jnp.bfloat16)


def split3(value):
    high = value.astype(jnp.bfloat16)
    rest = value - high.astype(jnp.float32)
    middle = rest.astype(jnp.bfloat16)
    return high, middle, (rest - middle.astype(jnp.float32)).astype(jnp.bfloat16)


def dot_split(a, b, dims=NN):
    return dot(a[0], b[0], dims) + (dot(a[0], b[1], dims) + dot(a[1], b[0], dims))


def mixing_matrices():
    parts = []
    for matrix, gain in ((EVEN, None), (ODD, None), (EVEN, EVEN_GAIN), (ODD, ODD_GAIN)):
        matrix = np.array(matrix)
        if gain is not None:
            matrix = matrix / np.array(gain)[:, None]
        rest = np.pad(matrix, ((0, 16 - RANK), (0, 0))).astype(np.float32)
        pieces = []
        for _ in range(3):
            pieces.append(rest.astype(jnp.bfloat16))
            rest = rest - pieces[-1].astype(np.float32)
        first, second, third = pieces
        row = np.concatenate([first, first, second, second, first, third], axis=1)
        parts.append(np.pad(row, ((0, 0), (0, 128 - row.shape[1]))))
    return np.concatenate(parts, axis=1).astype(np.float32)


def mix(matrix, value):
    high, middle, low = split3(value)
    return dot(matrix, jnp.concatenate([high, middle, high, middle, low, high], axis=0))


def factors(first, second, mixing):
    width = first.shape[1]
    index = lax.broadcasted_iota(jnp.int32, (16, 1), 0)
    nodes = jnp.zeros((16, 1), jnp.float32)
    for i, node in enumerate(NODES):
        nodes = jnp.where(index == i, node, nodes)
    cos_part, sin_part = cos_sin(nodes * jnp.concatenate([first, second], axis=1))
    evens = mix(mixing[:, :96], cos_part)
    odds = mix(mixing[:, 128:224], sin_part)
    return evens[:, :width], odds[:, :width], evens[:, width:], odds[:, width:]


def outer_rows(left, right):
    for i in range(0, RANK, 2):
        yield jnp.concatenate([left[:8] * right[i : i + 1], left[:8] * right[i + 1 : i + 2]], axis=0)
    for i in range(8, RANK, 2):
        yield jnp.concatenate([left[i : i + 1] * right[:8], left[i + 1 : i + 2] * right[:8]], axis=0)


PAIR_ROWS = 8 * RANK + 8 * (RANK - 8)


def store_rows(high, low, columns, evx, odx, evy, ody, is_cos, sign):
    pairs = ((evx, evy, 1.0), (odx, ody, sign)) if is_cos else ((odx, evy, 1.0), (evx, ody, 1.0))
    row = 0
    for left, right, factor in pairs:
        if factor < 0:
            right = -right
        for value in outer_rows(left, right):
            part = split(value)
            high[row : row + 16, columns] = part[0]
            low[row : row + 16, columns] = part[1]
            row += 16


def as_column(row):
    count = row.shape[1]
    here = lax.broadcasted_iota(jnp.int32, (count, count), 0)
    there = lax.broadcasted_iota(jnp.int32, (count, count), 1)
    return jnp.sum(jnp.where(here == there, row, 0.0), axis=1, keepdims=True)


def structure_kernel(
    sizes, density_far, packed,
    partial, cos_out, sin_out, wave_c_high, wave_c_low, wave_s_high, wave_s_low,
    point_c_high, point_c_low, point_s_high, point_s_low,
    density, form_c, form_s, arrived,
):
    copy = pltpu.make_async_copy(density_far, density, arrived)
    copy.start()
    views, start = [], 0
    for size in sizes:
        padded = -(-size // 128) * 128
        views.append(packed.at[:, start : start + padded])
        start += padded
    waves, points, centers, mixing = views
    mixing = mixing[...].astype(jnp.bfloat16)
    every = slice(None)
    scale = 2.0 * BAND * TURN
    parts = factors(points[0:1, :] * scale, points[1:2, :] * scale, mixing[:, :256])
    store_rows(point_c_high, point_c_low, every, *parts, True, -1.0)
    store_rows(point_s_high, point_s_low, every, *parts, False, 1.0)
    copy.wait()
    dens = density[...]
    held_c = split(dot(dens, point_c_high[...], NT) + dot(dens, point_c_low[...], NT))
    held_s = split(dot(dens, point_s_high[...], NT) + dot(dens, point_s_low[...], NT))
    center_x = as_column(centers[0:1, :][:, : density.shape[0]])
    center_y = as_column(centers[1:2, :][:, : density.shape[0]])
    atoms, modes = cos_out.shape
    tile = min(MODE_TILE, modes)
    for start in range(0, modes, tile):
        here = slice(start, start + tile)
        kx = waves[0:1, here] * TURN
        ky = waves[1:2, here] * TURN
        parts = factors(kx * (BAND / 24.0), ky * (BAND / 24.0), mixing[:, 256:])
        store_rows(wave_c_high, wave_c_low, here, *parts, True, 1.0)
        store_rows(wave_s_high, wave_s_low, here, *parts, False, 1.0)
        form_c[:, here] = dot_split(held_c, (wave_c_high[:, here], wave_c_low[:, here]))
        form_s[:, here] = dot_split(held_s, (wave_s_high[:, here], wave_s_low[:, here]))
        real = jnp.zeros((16, tile), jnp.float32)
        imag = jnp.zeros((16, tile), jnp.float32)
        for row in range(0, atoms, 16):
            rows = slice(row, row + 16)
            cos_c, sin_c = cos_sin(center_x[rows] * kx + center_y[rows] * ky)
            cos_out[rows, here] = cos_c
            sin_out[rows, here] = sin_c
            cos_f, sin_f = form_c[rows, here], form_s[rows, here]
            real = real + (cos_c * cos_f - sin_c * sin_f)
            imag = imag + (sin_c * cos_f + cos_c * sin_f)
        partial[0:1, here] = jnp.sum(real, axis=0, keepdims=True)
        partial[1:2, here] = -jnp.sum(imag, axis=0, keepdims=True)


def partial_structure(density, centers, points, waves):
    atoms, count = density.shape
    modes = waves.shape[1]
    rows = 2 * PAIR_ROWS
    bf16, f32 = jnp.bfloat16, jnp.float32
    mixing = mixing_matrices()
    parts = [waves, points, centers, mixing]
    sizes = [part.shape[1] for part in parts]
    packed = jnp.concatenate(
        [jnp.pad(p, ((0, 16 - p.shape[0]), (0, -p.shape[1] % 128))) for p in parts], axis=1
    )
    out = lambda shape, kind: jax.ShapeDtypeStruct(shape, kind)
    return pl.pallas_call(
        functools.partial(structure_kernel, sizes),
        in_specs=[pl.BlockSpec(memory_space=pltpu.HBM), pl.BlockSpec(memory_space=pltpu.VMEM)],
        out_shape=[out((2, modes), f32)] + [out((atoms, modes), f32)] * 2
        + [out((rows, modes), bf16)] * 4 + [out((rows, count), bf16)] * 4,
        scratch_shapes=[pltpu.VMEM((atoms, count), bf16)]
        + [pltpu.VMEM((atoms, modes), f32)] * 2 + [pltpu.SemaphoreType.DMA],
        compiler_params=pltpu.CompilerParams(vmem_limit_bytes=30 * MIB),
        cost_estimate=pl.CostEstimate(
            flops=16 * atoms * rows * (count * 4 + modes * 6),
            bytes_accessed=8 * atoms * modes, transcendentals=0,
        ),
    )(density, packed)


def far_kernel(
    normalizer, first, second, weight, cos_c, sin_c,
    wave_c_high, wave_c_low, wave_s_high, wave_s_low,
    point_c_high, point_c_low, point_s_high, point_s_low,
    keep, send, spread_c_high, spread_c_low, spread_s_high, spread_s_low, field,
):
    atoms, modes = cos_c.shape
    tile = min(MODE_TILE, modes)
    held_c = held_s = None
    for start in range(0, modes, tile):
        here = slice(start, start + tile)
        scaled = weight[:, here] * normalizer
        real = (first[0:1, here] + second[0:1, here]) * scaled
        imag = (first[1:2, here] + second[1:2, here]) * scaled
        for row in range(0, atoms, 16):
            rows = slice(row, row + 16)
            cosine, sine = cos_c[rows, here], sin_c[rows, here]
            spread_c_high[rows, here], spread_c_low[rows, here] = split(real * cosine - imag * sine)
            spread_s_high[rows, here], spread_s_low[rows, here] = split(-(real * sine + imag * cosine))
        part_c = dot_split(
            (spread_c_high[:, here], spread_c_low[:, here]),
            (wave_c_high[:, here], wave_c_low[:, here]), NT,
        )
        part_s = dot_split(
            (spread_s_high[:, here], spread_s_low[:, here]),
            (wave_s_high[:, here], wave_s_low[:, here]), NT,
        )
        held_c = part_c if held_c is None else held_c + part_c
        held_s = part_s if held_s is None else held_s + part_s
    field[...] = dot_split(
        split(held_c), (point_c_high[...], point_c_low[...])
    ) + dot_split(split(held_s), (point_s_high[...], point_s_low[...]))
    chip, core = lax.axis_index("z_lo"), lax.axis_index("core")
    chips, _, width = keep.shape
    for ahead in range(chips):
        other = jnp.bitwise_xor(chip, ahead)
        mine = pl.multiple_of((2 * other + core) * width, width)
        theirs = pl.multiple_of((2 * other + 1 - core) * width, width)
        keep[ahead] = field[:, pl.ds(mine, width)]
        send[ahead] = field[:, pl.ds(theirs, width)]


def far_partial(normalizer, first, second, weight, cos_c, sin_c, waves, points, chips):
    atoms, modes = cos_c.shape
    rows, count = points[0].shape
    width = count // (2 * chips)
    return pl.pallas_call(
        functools.partial(far_kernel, normalizer),
        out_shape=[jax.ShapeDtypeStruct((chips, atoms, width), jnp.float32)] * 2,
        scratch_shapes=[pltpu.VMEM((atoms, modes), jnp.bfloat16)] * 4
        + [pltpu.VMEM((atoms, count), jnp.float32)],
        compiler_params=pltpu.CompilerParams(vmem_limit_bytes=30 * MIB),
        cost_estimate=pl.CostEstimate(
            flops=2 * atoms * rows * 6 * (count + modes),
            bytes_accessed=8 * atoms * modes, transcendentals=0,
        ),
    )(first, second, weight, cos_c, sin_c, *waves, *points)


def near_kernel(group, is_halo, offsets, atoms_of, counts, near, start, *rest):
    given, (out, sources, values, picks, made) = rest[:-5], rest[-5:]
    classes, width, count = near.shape
    atoms = out.shape[0]
    used = atoms * len(given)
    wide = picks.shape[2] // group
    for i, block in enumerate(given):
        sources[i * atoms : (i + 1) * atoms, :] = block[...]
    core = lax.axis_index("core")
    blocks = lax.axis_size(BLOCK_AXES)
    shift = atoms_of[...] - (lax.axis_index(BLOCK_AXES) - 1) * atoms
    shift = jnp.where(shift < 0, shift + blocks * atoms, shift)
    shift = jnp.where(shift >= blocks * atoms, shift - blocks * atoms, shift)
    live = lax.broadcasted_iota(jnp.int32, shift.shape, 0) < counts[...]
    places = jnp.where(live, shift + 1, 0).astype(jnp.float32)
    of_slot = offsets[...]
    found = [
        jnp.sum(jnp.where(of_slot == one, places, 0.0), axis=0, keepdims=True)
        for one in range(classes)
    ]
    found.append(jnp.zeros((-classes % 8, atoms), jnp.float32))
    found = jnp.transpose(jnp.concatenate(found, axis=0))
    column = lax.broadcasted_iota(jnp.int32, (1, wide), 1)
    if is_halo:
        base = jnp.where(column < atoms, core * 2 * atoms, (1 - core) * 2 * atoms - atoms)
    else:
        base = atoms
    target = jnp.where(column < used, column + base + 1, -1).astype(jnp.float32)
    for slot in range(2):
        for one in range(group):
            values[slot, one * wide + used : (one + 1) * wide, :] = jnp.zeros(
                (wide - used, 2 * width), values.dtype
            )
    result = jnp.zeros((atoms, 2 * width), jnp.float32)
    steps = classes // group
    for step in range(steps + 1):
        slot = step % 2
        if step < steps:
            block = near[step * group : (step + 1) * group].reshape(group * width, count)
            made[slot] = dot(sources[...], block, NT)
            for one in range(group):
                own_class = step * group + one
                chosen = jnp.where(found[:, own_class : own_class + 1] == target, 1.0, 0.0)
                picks[slot, :, one * wide : (one + 1) * wide] = chosen.astype(jnp.bfloat16)
        if step > 0:
            result = result + dot(picks[1 - slot], values[1 - slot])
        if step < steps:
            for one in range(group):
                high, low = split(made[slot, :, one * width : (one + 1) * width])
                rows = slice(one * wide, one * wide + used)
                values[slot, rows, :width] = high
                values[slot, rows, width:] = low
    if is_halo:
        begin = start[...]
    else:
        member = lax.axis_index("z_lo") * 2 + core
        mine = pl.multiple_of(member * width, width)
        begin = 0.5 * start[:, pl.ds(mine, width)].astype(jnp.float32)
    out[...] = begin + (result[:, :width] + result[:, width:])


def near_part(is_halo, offsets, atoms_of, counts, near, start, given):
    atoms = offsets.shape[1]
    classes, width, count = near.shape
    group = CLASS_TILE if classes % CLASS_TILE == 0 else 1
    used = atoms * len(given)
    wide = -(-used // 128) * 128
    bf16, f32 = jnp.bfloat16, jnp.float32
    return pl.pallas_call(
        functools.partial(near_kernel, group, is_halo),
        scratch_shapes=[
            pltpu.VMEM((used, count), bf16), pltpu.VMEM((2, group * wide, 2 * width), bf16),
            pltpu.VMEM((2, atoms, group * wide), bf16), pltpu.VMEM((2, used, group * width), f32),
        ],
        out_shape=jax.ShapeDtypeStruct((atoms, width), f32),
        compiler_params=pltpu.CompilerParams(vmem_limit_bytes=30 * MIB),
        cost_estimate=pl.CostEstimate(
            flops=2 * used * classes * width * (count + 2 * atoms),
            bytes_accessed=2 * classes * width * count, transcendentals=0,
        ),
    )(offsets, atoms_of, counts, near, start, *given)


def fold_kernel(keep, taken, *outs):
    for ahead, out in enumerate(outs):
        out[...] = keep[ahead] + taken[ahead]


def fold(keep, taken):
    chips, atoms, width = keep.shape
    return pl.pallas_call(
        fold_kernel,
        out_shape=[jax.ShapeDtypeStruct((atoms, width), jnp.float32)] * chips,
        compiler_params=pltpu.CompilerParams(vmem_limit_bytes=8 * MIB),
    )(keep, taken)


def shifted(value, axis, by):
    count = lax.axis_size(axis)
    return lax.ppermute(value, axis, [(i, (i + by) % count) for i in range(count)])


def sum_over(value, axis):
    count = lax.axis_size(axis)
    return value + sum(shifted(value, axis, by) for by in range(1, count))


def shards(
    density, near_blocks, neighbour_atoms, neighbour_offsets, neighbour_counts,
    centers, local_points, wavevectors, spectral_weight,
):
    atoms, points = density.shape
    blocks = lax.axis_size(BLOCK_AXES)
    modes = wavevectors.shape[1]
    chips, cores = lax.axis_size("z_lo"), lax.axis_size("core")
    normalizer = 1.0 / math.sqrt(atoms * blocks * points * modes * chips * cores)

    halo_route = []
    ring = lax.axis_size("y")
    for source in range(blocks):
        for chip in range(chips):
            for core, target in ((0, (source + 1) % blocks), (1, (source - 1) % blocks)):
                to = chip if source // ring == target // ring else chips - 1 - chip
                halo_route.append(((source * chips + chip) * 2 + core, (target * chips + to) * 2 + core))
    halo = lax.ppermute(density, BLOCK_AXES + ("z_lo", "core"), halo_route)

    partial, cos_c, sin_c, *tables = partial_structure(density, centers, local_points, wavevectors)

    lists = (neighbour_offsets.T, neighbour_atoms.T, neighbour_counts[None, :])
    near_own = near_part(False, *lists, near_blocks, density, [density])

    structure = sum_over(partial, "y")
    structure = sum_over(structure, "x")
    other_half = shifted(structure, "z_hi", 1)
    halo_other = lax.ppermute(halo, "core", [(0, 1), (1, 0)])

    structure, near_own = lax.optimization_barrier((structure, near_own))
    keep, send = far_partial(
        normalizer, structure, other_half, spectral_weight[None, :], cos_c, sin_c,
        tables[:4], tables[4:], chips,
    )
    taken = lax.ppermute(send, "core", [(0, 1), (1, 0)])
    near_field = near_part(True, *lists, near_blocks, near_own, [halo, halo_other])
    pieces = fold(keep, taken)
    far_field = pieces[0]
    for by in range(1, chips):
        swap = [(i, i ^ by) for i in range(chips)]
        far_field = far_field + lax.ppermute(pieces[by], "z_lo", swap)
    return near_field + far_field


def solution(mesh):
    fine = Mesh(
        mesh.devices.reshape(4, 2, 4, 4, 2), ("x", "z_hi", "y", "z_lo", "core")
    )
    modes = ("z_lo", "core")
    placed = (
        P(BLOCK_AXES, None), P(None, modes, None), P(BLOCK_AXES, None), P(BLOCK_AXES, None),
        P(BLOCK_AXES), P(None, BLOCK_AXES), P(), P(None, modes), P(modes),
    )
    return jax.shard_map(
        shards, mesh=fine, in_specs=placed, out_specs=P(BLOCK_AXES, modes), check_vma=False
    )
```

```python
import functools
import math

import jax
import jax.numpy as jnp
import numpy as np
from jax import lax
from jax.experimental import pallas as pl
from jax.experimental.pallas import tpu as pltpu
from jax.sharding import Mesh
from jax.sharding import PartitionSpec as P

BAND = 12.0
NODES = (
    0.04830766569, 0.1444719616, 0.2392873623, 0.3318686023, 0.4213512761, 0.5068999089, 0.5877157572, 0.6630442669, 0.7321821187, 0.794483796, 0.8493676137, 0.8963211558, 0.9349060759, 0.9647622556, 0.9856115115, 0.9972638618,
)
EVEN = (
    (0.264161544, 0.235683413, 0.1877892764, 0.1338856267, 0.08565638585, 0.04935936307, 0.02573553405, 0.01220462496, 0.005294905203, 0.00211445586, 0.0007820202318, 0.0002693802975, 8.679038294e-05, 2.6181341e-05, 7.331099629e-06, 1.708479253e-06),
    (0.1702613529, 0.08465650818, -0.04082940747, -0.1469360259, -0.1970030198, -0.1901061112, -0.1489564192, -0.09954602317, -0.05833865755, -0.03055765255, -0.01451635874, -0.006328267813, -0.002555179594, -0.0009609245647, -0.000333851875, -9.333966862e-05),
    (-0.1323973182, -0.02247601982, 0.1047497372, 0.1503633392, 0.08986991162, -0.02455938248, -0.1219371619, -0.1640572477, -0.1545048367, -0.1178161583, -0.07717100148, -0.0448976056, -0.02371842969, -0.01152257368, -0.005081924909, -0.001704677766),
    (-0.1038663831, 0.008772611212, 0.1112611228, 0.09900945939, -0.007887275225, -0.1049440761, -0.1157944762, -0.04697227583, 0.04443730952, 0.108316557, 0.1285622126, 0.1155652092, 0.08749662772, 0.05797221816, 0.03303595529, 0.01312861586),
    (-0.09524794649, 0.02681958951, 0.1142235556, 0.06137473355, -0.06159895528, -0.114537939, -0.05174444256, 0.05425346059, 0.1112188114, 0.08907465173, 0.01933187924, -0.05021028773, -0.08987667008, -0.09410761546, -0.0713193742, -0.03310624913),
    (0.1022051591, -0.05281704117, -0.1277713562, -0.0158252522, 0.116158395, 0.09060969529, -0.0463884297, -0.1239497875, -0.06822339825, 0.04641750905, 0.1115635062, 0.08861974282, 0.01440006111, -0.05133346873, -0.07076867034, -0.04114204128),
    (-0.1016349432, 0.081731359, 0.1180899649, -0.05213972209, -0.1310463958, 0.004828729775, 0.1285200703, 0.06026154641, -0.08513107212, -0.1134175056, -0.009982527353, 0.09053034847, 0.0894231339, 0.01200695961, -0.051135621, -0.04311496388),
    (-0.09691907606, 0.1086033655, 0.08463923718, -0.1138806091, -0.07938954229, 0.1091864505, 0.0866221684, -0.08980194788, -0.1037585862, 0.04854215716, 0.1134990489, 0.01271606801, -0.08781269714, -0.0609974537, 0.02562700126, 0.04324151356),
    (-0.08972912127, 0.1300425509, 0.03237330507, -0.1418919531, 0.02055363161, 0.132001602, -0.05367707241, -0.1161966312, 0.06348478865, 0.1052884638, -0.05273929295, -0.09804759123, 0.02676341234, 0.0825150306, 0.001318540609, -0.04206423821),
    (-0.0807528844, 0.1433856071, -0.02927536699, -0.1203274859, 0.113532529, 0.04297640002, -0.1359071454, 0.03217281435, 0.1131044363, -0.07497313561, -0.07767707065, 0.08565207726, 0.04832778656, -0.07373331536, -0.0262794175, 0.03977430954),
)
ODD = (
    (-0.06039643671, -0.1619285065, -0.2157655924, -0.2164663713, -0.179285157, -0.1273735765, -0.07932182359, -0.04395383706, -0.0219317145, -0.009956138688, -0.004149848215, -0.001600910605, -0.0005751981407, -0.0001930716936, -6.006259695e-05, -1.532579998e-05),
    (0.06770405989, 0.1570721263, 0.1434280287, 0.04295191184, -0.07879962265, -0.1610074452, -0.1820744199, -0.1564850599, -0.1117106857, -0.06911197019, -0.03803899989, -0.018976138, -0.008700246907, -0.003698004317, -0.001443221181, -0.0004421770918),
    (-0.06672308627, -0.1353009509, -0.07559650806, 0.05145652305, 0.1328476776, 0.1110923906, 0.01620622731, -0.08318512773, -0.1393111579, -0.1451173835, -0.1191406959, -0.08344766078, -0.05189716398, -0.02921471538, -0.01463357191, -0.005358686102),
    (-0.06188570509, -0.1120544487, -0.03164468805, 0.08318098917, 0.1076065769, 0.02554639647, -0.07633334629, -0.1130798134, -0.07076087078, 0.008202589998, 0.07547632887, 0.1077871043, 0.1068753005, 0.08546497618, 0.0555295236, 0.02380489812),
    (0.07294621453, 0.1170272587, 0.0005822684711, -0.1151664239, -0.08239886349, 0.04808258285, 0.1205972232, 0.06802484515, -0.04264531193, -0.1109041826, -0.09690224579, -0.0289313287, 0.0417153054, 0.07952536804, 0.07530043037, 0.03856509779),
    (0.08652145766, 0.1159240548, -0.04433348034, -0.1318825677, -0.0146605442, 0.1210590442, 0.0842447592, -0.05956973628, -0.1239316034, -0.0494564638, 0.06563154857, 0.1089604688, 0.06071412772, -0.01917666675, -0.06207287706, -0.04244003862),
    (0.09796928773, 0.1014768063, -0.091850156, -0.1080980874, 0.07605361357, 0.1198048209, -0.04229231028, -0.1286411677, -0.01461539232, 0.1112662457, 0.07892093947, -0.04457606115, -0.09810478366, -0.03937820657, 0.03879814661, 0.04335854939),
    (0.1083285032, 0.07708721735, -0.1285703026, -0.0450395491, 0.1354076647, 0.02413735124, -0.1328629117, -0.02187888439, 0.1235455303, 0.03873152733, -0.1025408614, -0.0647085451, 0.06221363399, 0.07559191195, -0.01210690766, -0.04280157103),
    (0.1177268554, 0.04504968521, -0.1441555522, 0.03839419971, 0.1212170689, -0.09675550887, -0.07572314606, 0.120135559, 0.03631601591, -0.1190390193, -0.01579049946, 0.1052262271, 0.01219152635, -0.08172301286, -0.01423910674, 0.04104943366),
    (0.126120285, 0.007979130802, -0.1328480522, 0.1116338241, 0.03421605314, -0.1374354291, 0.07279981158, 0.07996744654, -0.1205095327, -0.004441967651, 0.111290914, -0.04516234118, -0.07618300914, 0.05955705328, 0.03710370067, -0.03825468552),
)
EVEN_GAIN = (
    0.7236012542, -0.7236000597, 0.7230899637, -0.6794753044, 0.309908605, -0.04203461377, 0.003110230195, -0.0001597812355, 6.121678833e-06, -1.82449892e-07,
)
ODD_GAIN = (
    0.7236012257, -0.7235710907, 0.7176666509, -0.5402161025, 0.127514432, -0.01205222733, 0.0007337517912, -3.234542573e-05, 1.088270167e-06, -2.894614862e-08,
)
RANK = 10
TURN = 1.0 / (2.0 * math.pi)
SIN_COEFS = (
    6.283182818550517, -41.3414213986335, 81.59618387150637,
    -76.58010050946145, 41.20539479011024, -12.271262230884131,
)
COS_COEFS = (
    0.9999999891722597, -19.739204532088525, 64.93911898360994, -85.45016554540021,
    60.167831693053074, -25.96831316496443, 6.52961023180932,
)
MODE_TILE = 512
CLASS_TILE = 9
NT = (((1,), (1,)), ((), ()))
NN = (((1,), (0,)), ((), ()))
BLOCK_AXES = ("x", "z_hi", "y")
MIB = 1024 * 1024


def horner(coefs, square):
    total = jnp.full_like(square, coefs[-1])
    for coef in coefs[-2::-1]:
        total = total * square + coef
    return total


def cos_sin(turns):
    rest = turns - jnp.round(turns)
    square = rest * rest
    return horner(COS_COEFS, square), rest * horner(SIN_COEFS, square)


def dot(a, b, dims=NN):
    return lax.dot_general(a, b, dims, preferred_element_type=jnp.float32)


def split(value):
    high = value.astype(jnp.bfloat16)
    return high, (value - high.astype(jnp.float32)).astype(jnp.bfloat16)


def split3(value):
    high = value.astype(jnp.bfloat16)
    rest = value - high.astype(jnp.float32)
    middle = rest.astype(jnp.bfloat16)
    return high, middle, (rest - middle.astype(jnp.float32)).astype(jnp.bfloat16)


def dot_split(a, b, dims=NN):
    return dot(a[0], b[0], dims) + (dot(a[0], b[1], dims) + dot(a[1], b[0], dims))


def mixing_matrices():
    parts = []
    for matrix, gain in ((EVEN, None), (ODD, None), (EVEN, EVEN_GAIN), (ODD, ODD_GAIN)):
        matrix = np.array(matrix)
        if gain is not None:
            matrix = matrix / np.array(gain)[:, None]
        rest = np.pad(matrix, ((0, 16 - RANK), (0, 0))).astype(np.float32)
        pieces = []
        for _ in range(3):
            pieces.append(rest.astype(jnp.bfloat16))
            rest = rest - pieces[-1].astype(np.float32)
        first, second, third = pieces
        row = np.concatenate([first, first, second, second, first, third], axis=1)
        parts.append(np.pad(row, ((0, 0), (0, 128 - row.shape[1]))))
    return np.concatenate(parts, axis=1).astype(np.float32)


def mix(matrix, value):
    high, middle, low = split3(value)
    return dot(matrix, jnp.concatenate([high, middle, high, middle, low, high], axis=0))


def factors(first, second, mixing):
    width = first.shape[1]
    index = lax.broadcasted_iota(jnp.int32, (16, 1), 0)
    nodes = jnp.zeros((16, 1), jnp.float32)
    for i, node in enumerate(NODES):
        nodes = jnp.where(index == i, node, nodes)
    cos_part, sin_part = cos_sin(nodes * jnp.concatenate([first, second], axis=1))
    evens = mix(mixing[:, :96], cos_part)
    odds = mix(mixing[:, 128:224], sin_part)
    return evens[:, :width], odds[:, :width], evens[:, width:], odds[:, width:]


def outer_rows(left, right):
    for i in range(0, RANK, 2):
        yield jnp.concatenate([left[:8] * right[i : i + 1], left[:8] * right[i + 1 : i + 2]], axis=0)
    for i in range(8, RANK, 2):
        yield jnp.concatenate([left[i : i + 1] * right[:8], left[i + 1 : i + 2] * right[:8]], axis=0)


PAIR_ROWS = 8 * RANK + 8 * (RANK - 8)


def store_rows(high, low, columns, evx, odx, evy, ody, is_cos, sign):
    pairs = ((evx, evy, 1.0), (odx, ody, sign)) if is_cos else ((odx, evy, 1.0), (evx, ody, 1.0))
    row = 0
    for left, right, factor in pairs:
        if factor < 0:
            right = -right
        for value in outer_rows(left, right):
            part = split(value)
            high[row : row + 16, columns] = part[0]
            low[row : row + 16, columns] = part[1]
            row += 16


def as_column(row):
    count = row.shape[1]
    here = lax.broadcasted_iota(jnp.int32, (count, count), 0)
    there = lax.broadcasted_iota(jnp.int32, (count, count), 1)
    return jnp.sum(jnp.where(here == there, row, 0.0), axis=1, keepdims=True)


def structure_kernel(
    sizes, density_far, packed,
    partial, cos_out, sin_out, wave_c_high, wave_c_low, wave_s_high, wave_s_low,
    point_c_high, point_c_low, point_s_high, point_s_low,
    density, form_c, form_s, arrived,
):
    copy = pltpu.make_async_copy(density_far, density, arrived)
    copy.start()
    views, start = [], 0
    for size in sizes:
        padded = -(-size // 128) * 128
        views.append(packed.at[:, start : start + padded])
        start += padded
    waves, points, centers, mixing = views
    mixing = mixing[...].astype(jnp.bfloat16)
    every = slice(None)
    scale = 2.0 * BAND * TURN
    parts = factors(points[0:1, :] * scale, points[1:2, :] * scale, mixing[:, :256])
    store_rows(point_c_high, point_c_low, every, *parts, True, -1.0)
    store_rows(point_s_high, point_s_low, every, *parts, False, 1.0)
    copy.wait()
    dens = density[...]
    held_c = split(dot(dens, point_c_high[...], NT) + dot(dens, point_c_low[...], NT))
    held_s = split(dot(dens, point_s_high[...], NT) + dot(dens, point_s_low[...], NT))
    center_x = as_column(centers[0:1, :][:, : density.shape[0]])
    center_y = as_column(centers[1:2, :][:, : density.shape[0]])
    atoms, modes = cos_out.shape
    tile = min(MODE_TILE, modes)
    for start in range(0, modes, tile):
        here = slice(start, start + tile)
        kx = waves[0:1, here] * TURN
        ky = waves[1:2, here] * TURN
        parts = factors(kx * (BAND / 24.0), ky * (BAND / 24.0), mixing[:, 256:])
        store_rows(wave_c_high, wave_c_low, here, *parts, True, 1.0)
        store_rows(wave_s_high, wave_s_low, here, *parts, False, 1.0)
        form_c[:, here] = dot_split(held_c, (wave_c_high[:, here], wave_c_low[:, here]))
        form_s[:, here] = dot_split(held_s, (wave_s_high[:, here], wave_s_low[:, here]))
        real = jnp.zeros((16, tile), jnp.float32)
        imag = jnp.zeros((16, tile), jnp.float32)
        for row in range(0, atoms, 16):
            rows = slice(row, row + 16)
            cos_c, sin_c = cos_sin(center_x[rows] * kx + center_y[rows] * ky)
            cos_out[rows, here] = cos_c
            sin_out[rows, here] = sin_c
            cos_f, sin_f = form_c[rows, here], form_s[rows, here]
            real = real + (cos_c * cos_f - sin_c * sin_f)
            imag = imag + (sin_c * cos_f + cos_c * sin_f)
        partial[0:1, here] = jnp.sum(real, axis=0, keepdims=True)
        partial[1:2, here] = -jnp.sum(imag, axis=0, keepdims=True)


def partial_structure(density, centers, points, waves):
    atoms, count = density.shape
    modes = waves.shape[1]
    rows = 2 * PAIR_ROWS
    bf16, f32 = jnp.bfloat16, jnp.float32
    mixing = mixing_matrices()
    parts = [waves, points, centers, mixing]
    sizes = [part.shape[1] for part in parts]
    packed = jnp.concatenate(
        [jnp.pad(p, ((0, 16 - p.shape[0]), (0, -p.shape[1] % 128))) for p in parts], axis=1
    )
    out = lambda shape, kind: jax.ShapeDtypeStruct(shape, kind)
    return pl.pallas_call(
        functools.partial(structure_kernel, sizes),
        in_specs=[pl.BlockSpec(memory_space=pltpu.HBM), pl.BlockSpec(memory_space=pltpu.VMEM)],
        out_shape=[out((2, modes), f32)] + [out((atoms, modes), f32)] * 2
        + [out((rows, modes), bf16)] * 4 + [out((rows, count), bf16)] * 4,
        scratch_shapes=[pltpu.VMEM((atoms, count), bf16)]
        + [pltpu.VMEM((atoms, modes), f32)] * 2 + [pltpu.SemaphoreType.DMA],
        compiler_params=pltpu.CompilerParams(vmem_limit_bytes=30 * MIB),
        cost_estimate=pl.CostEstimate(
            flops=16 * atoms * rows * (count * 4 + modes * 6),
            bytes_accessed=8 * atoms * modes, transcendentals=0,
        ),
    )(density, packed)


def far_kernel(
    normalizer, first, second, weight, cos_c, sin_c,
    wave_c_high, wave_c_low, wave_s_high, wave_s_low,
    point_c_high, point_c_low, point_s_high, point_s_low,
    keep, send, spread_c_high, spread_c_low, spread_s_high, spread_s_low, field,
):
    atoms, modes = cos_c.shape
    tile = min(MODE_TILE, modes)
    held_c = held_s = None
    for start in range(0, modes, tile):
        here = slice(start, start + tile)
        scaled = weight[:, here] * normalizer
        real = (first[0:1, here] + second[0:1, here]) * scaled
        imag = (first[1:2, here] + second[1:2, here]) * scaled
        for row in range(0, atoms, 16):
            rows = slice(row, row + 16)
            cosine, sine = cos_c[rows, here], sin_c[rows, here]
            spread_c_high[rows, here], spread_c_low[rows, here] = split(real * cosine - imag * sine)
            spread_s_high[rows, here], spread_s_low[rows, here] = split(-(real * sine + imag * cosine))
        part_c = dot_split(
            (spread_c_high[:, here], spread_c_low[:, here]),
            (wave_c_high[:, here], wave_c_low[:, here]), NT,
        )
        part_s = dot_split(
            (spread_s_high[:, here], spread_s_low[:, here]),
            (wave_s_high[:, here], wave_s_low[:, here]), NT,
        )
        held_c = part_c if held_c is None else held_c + part_c
        held_s = part_s if held_s is None else held_s + part_s
    field[...] = dot_split(
        split(held_c), (point_c_high[...], point_c_low[...])
    ) + dot_split(split(held_s), (point_s_high[...], point_s_low[...]))
    chip, core = lax.axis_index("z_lo"), lax.axis_index("core")
    chips, _, width = keep.shape
    for ahead in range(chips):
        other = jnp.bitwise_xor(chip, ahead)
        mine = pl.multiple_of((2 * other + core) * width, width)
        theirs = pl.multiple_of((2 * other + 1 - core) * width, width)
        keep[ahead] = field[:, pl.ds(mine, width)]
        send[ahead] = field[:, pl.ds(theirs, width)]


def far_partial(normalizer, first, second, weight, cos_c, sin_c, waves, points, chips):
    atoms, modes = cos_c.shape
    rows, count = points[0].shape
    width = count // (2 * chips)
    return pl.pallas_call(
        functools.partial(far_kernel, normalizer),
        out_shape=[jax.ShapeDtypeStruct((chips, atoms, width), jnp.float32)] * 2,
        scratch_shapes=[pltpu.VMEM((atoms, modes), jnp.bfloat16)] * 4
        + [pltpu.VMEM((atoms, count), jnp.float32)],
        compiler_params=pltpu.CompilerParams(vmem_limit_bytes=30 * MIB),
        cost_estimate=pl.CostEstimate(
            flops=2 * atoms * rows * 6 * (count + modes),
            bytes_accessed=8 * atoms * modes, transcendentals=0,
        ),
    )(first, second, weight, cos_c, sin_c, *waves, *points)


def near_kernel(group, is_halo, offsets, atoms_of, counts, near, start, *rest):
    given, (out, sources, values, picks, made) = rest[:-5], rest[-5:]
    classes, width, count = near.shape
    atoms = out.shape[0]
    used = atoms * len(given)
    wide = picks.shape[2] // group
    for i, block in enumerate(given):
        sources[i * atoms : (i + 1) * atoms, :] = block[...]
    core = lax.axis_index("core")
    blocks = lax.axis_size(BLOCK_AXES)
    shift = atoms_of[...] - (lax.axis_index(BLOCK_AXES) - 1) * atoms
    shift = jnp.where(shift < 0, shift + blocks * atoms, shift)
    shift = jnp.where(shift >= blocks * atoms, shift - blocks * atoms, shift)
    live = lax.broadcasted_iota(jnp.int32, shift.shape, 0) < counts[...]
    places = jnp.where(live, shift + 1, 0).astype(jnp.float32)
    of_slot = offsets[...]
    found = [
        jnp.sum(jnp.where(of_slot == one, places, 0.0), axis=0, keepdims=True)
        for one in range(classes)
    ]
    found.append(jnp.zeros((-classes % 8, atoms), jnp.float32))
    found = jnp.transpose(jnp.concatenate(found, axis=0))
    column = lax.broadcasted_iota(jnp.int32, (1, wide), 1)
    if is_halo:
        base = jnp.where(column < atoms, core * 2 * atoms, (1 - core) * 2 * atoms - atoms)
    else:
        base = atoms
    target = jnp.where(column < used, column + base + 1, -1).astype(jnp.float32)
    for slot in range(2):
        for one in range(group):
            values[slot, one * wide + used : (one + 1) * wide, :] = jnp.zeros(
                (wide - used, 2 * width), values.dtype
            )
    result = jnp.zeros((atoms, 2 * width), jnp.float32)
    steps = classes // group
    for step in range(steps + 1):
        slot = step % 2
        if step < steps:
            block = near[step * group : (step + 1) * group].reshape(group * width, count)
            made[slot] = dot(sources[...], block, NT)
            for one in range(group):
                own_class = step * group + one
                chosen = jnp.where(found[:, own_class : own_class + 1] == target, 1.0, 0.0)
                picks[slot, :, one * wide : (one + 1) * wide] = chosen.astype(jnp.bfloat16)
        if step > 0:
            result = result + dot(picks[1 - slot], values[1 - slot])
        if step < steps:
            for one in range(group):
                high, low = split(made[slot, :, one * width : (one + 1) * width])
                rows = slice(one * wide, one * wide + used)
                values[slot, rows, :width] = high
                values[slot, rows, width:] = low
    if is_halo:
        begin = start[...]
    else:
        member = lax.axis_index("z_lo") * 2 + core
        mine = pl.multiple_of(member * width, width)
        begin = 0.5 * start[:, pl.ds(mine, width)].astype(jnp.float32)
    out[...] = begin + (result[:, :width] + result[:, width:])


def near_part(is_halo, offsets, atoms_of, counts, near, start, given):
    atoms = offsets.shape[1]
    classes, width, count = near.shape
    group = CLASS_TILE if classes % CLASS_TILE == 0 else 1
    used = atoms * len(given)
    wide = -(-used // 128) * 128
    bf16, f32 = jnp.bfloat16, jnp.float32
    return pl.pallas_call(
        functools.partial(near_kernel, group, is_halo),
        scratch_shapes=[
            pltpu.VMEM((used, count), bf16), pltpu.VMEM((2, group * wide, 2 * width), bf16),
            pltpu.VMEM((2, atoms, group * wide), bf16), pltpu.VMEM((2, used, group * width), f32),
        ],
        out_shape=jax.ShapeDtypeStruct((atoms, width), f32),
        compiler_params=pltpu.CompilerParams(vmem_limit_bytes=30 * MIB),
        cost_estimate=pl.CostEstimate(
            flops=2 * used * classes * width * (count + 2 * atoms),
            bytes_accessed=2 * classes * width * count, transcendentals=0,
        ),
    )(offsets, atoms_of, counts, near, start, *given)


def fold_kernel(keep, taken, *outs):
    for ahead, out in enumerate(outs):
        out[...] = keep[ahead] + taken[ahead]


def fold(keep, taken):
    chips, atoms, width = keep.shape
    return pl.pallas_call(
        fold_kernel,
        out_shape=[jax.ShapeDtypeStruct((atoms, width), jnp.float32)] * chips,
        compiler_params=pltpu.CompilerParams(vmem_limit_bytes=8 * MIB),
    )(keep, taken)


def shifted(value, axis, by):
    count = lax.axis_size(axis)
    return lax.ppermute(value, axis, [(i, (i + by) % count) for i in range(count)])


def sum_over(value, axis):
    count = lax.axis_size(axis)
    return value + sum(shifted(value, axis, by) for by in range(1, count))


def shards(
    density, near_blocks, neighbour_atoms, neighbour_offsets, neighbour_counts,
    centers, local_points, wavevectors, spectral_weight,
):
    atoms, points = density.shape
    blocks = lax.axis_size(BLOCK_AXES)
    modes = wavevectors.shape[1]
    chips, cores = lax.axis_size("z_lo"), lax.axis_size("core")
    normalizer = 1.0 / math.sqrt(atoms * blocks * points * modes * chips * cores)

    halo_route = []
    ring = lax.axis_size("y")
    for source in range(blocks):
        for chip in range(chips):
            for core, target in ((0, (source + 1) % blocks), (1, (source - 1) % blocks)):
                to = chip if source // ring == target // ring else (chip + chips // 2) % chips
                halo_route.append(((source * chips + chip) * 2 + core, (target * chips + to) * 2 + core))
    halo = lax.ppermute(density, BLOCK_AXES + ("z_lo", "core"), halo_route)

    partial, cos_c, sin_c, *tables = partial_structure(density, centers, local_points, wavevectors)

    lists = (neighbour_offsets.T, neighbour_atoms.T, neighbour_counts[None, :])
    near_own = near_part(False, *lists, near_blocks, density, [density])

    structure = sum_over(partial, "y")
    structure = sum_over(structure, "x")
    other_half = shifted(structure, "z_hi", 1)
    halo_other = lax.ppermute(halo, "core", [(0, 1), (1, 0)])

    structure, near_own = lax.optimization_barrier((structure, near_own))
    keep, send = far_partial(
        normalizer, structure, other_half, spectral_weight[None, :], cos_c, sin_c,
        tables[:4], tables[4:], chips,
    )
    taken = lax.ppermute(send, "core", [(0, 1), (1, 0)])
    near_field = near_part(True, *lists, near_blocks, near_own, [halo, halo_other])
    far_field = keep[0] + taken[0]
    for by in range(chips - 1, 0, -1):
        swap = [(i, i ^ by) for i in range(chips)]
        piece = ((keep[by] + taken[by]) * (1.0 / 32.0)).astype(jnp.float16)
        far_field = far_field + lax.ppermute(piece, "z_lo", swap).astype(jnp.float32) * 32.0
    return near_field + far_field


def solution(mesh):
    fine = Mesh(
        mesh.devices.reshape(4, 2, 4, 4, 2), ("x", "z_hi", "y", "z_lo", "core")
    )
    modes = ("z_lo", "core")
    placed = (
        P(BLOCK_AXES, None), P(None, modes, None), P(BLOCK_AXES, None), P(BLOCK_AXES, None),
        P(BLOCK_AXES), P(None, BLOCK_AXES), P(), P(None, modes), P(modes),
    )
    return jax.shard_map(
        shards, mesh=fine, in_specs=placed, out_specs=P(BLOCK_AXES, modes), check_vma=False
    )
```

```python
import functools
import math

import jax
import jax.numpy as jnp
import numpy as np
from jax import lax
from jax.experimental import pallas as pl
from jax.experimental.pallas import tpu as pltpu
from jax.sharding import Mesh
from jax.sharding import PartitionSpec as P

BAND = 12.0
NODES = (
    0.04830766569, 0.1444719616, 0.2392873623, 0.3318686023, 0.4213512761, 0.5068999089, 0.5877157572, 0.6630442669, 0.7321821187, 0.794483796, 0.8493676137, 0.8963211558, 0.9349060759, 0.9647622556, 0.9856115115, 0.9972638618,
)
EVEN = (
    (0.264161544, 0.235683413, 0.1877892764, 0.1338856267, 0.08565638585, 0.04935936307, 0.02573553405, 0.01220462496, 0.005294905203, 0.00211445586, 0.0007820202318, 0.0002693802975, 8.679038294e-05, 2.6181341e-05, 7.331099629e-06, 1.708479253e-06),
    (0.1702613529, 0.08465650818, -0.04082940747, -0.1469360259, -0.1970030198, -0.1901061112, -0.1489564192, -0.09954602317, -0.05833865755, -0.03055765255, -0.01451635874, -0.006328267813, -0.002555179594, -0.0009609245647, -0.000333851875, -9.333966862e-05),
    (-0.1323973182, -0.02247601982, 0.1047497372, 0.1503633392, 0.08986991162, -0.02455938248, -0.1219371619, -0.1640572477, -0.1545048367, -0.1178161583, -0.07717100148, -0.0448976056, -0.02371842969, -0.01152257368, -0.005081924909, -0.001704677766),
    (-0.1038663831, 0.008772611212, 0.1112611228, 0.09900945939, -0.007887275225, -0.1049440761, -0.1157944762, -0.04697227583, 0.04443730952, 0.108316557, 0.1285622126, 0.1155652092, 0.08749662772, 0.05797221816, 0.03303595529, 0.01312861586),
    (-0.09524794649, 0.02681958951, 0.1142235556, 0.06137473355, -0.06159895528, -0.114537939, -0.05174444256, 0.05425346059, 0.1112188114, 0.08907465173, 0.01933187924, -0.05021028773, -0.08987667008, -0.09410761546, -0.0713193742, -0.03310624913),
    (0.1022051591, -0.05281704117, -0.1277713562, -0.0158252522, 0.116158395, 0.09060969529, -0.0463884297, -0.1239497875, -0.06822339825, 0.04641750905, 0.1115635062, 0.08861974282, 0.01440006111, -0.05133346873, -0.07076867034, -0.04114204128),
    (-0.1016349432, 0.081731359, 0.1180899649, -0.05213972209, -0.1310463958, 0.004828729775, 0.1285200703, 0.06026154641, -0.08513107212, -0.1134175056, -0.009982527353, 0.09053034847, 0.0894231339, 0.01200695961, -0.051135621, -0.04311496388),
    (-0.09691907606, 0.1086033655, 0.08463923718, -0.1138806091, -0.07938954229, 0.1091864505, 0.0866221684, -0.08980194788, -0.1037585862, 0.04854215716, 0.1134990489, 0.01271606801, -0.08781269714, -0.0609974537, 0.02562700126, 0.04324151356),
    (-0.08972912127, 0.1300425509, 0.03237330507, -0.1418919531, 0.02055363161, 0.132001602, -0.05367707241, -0.1161966312, 0.06348478865, 0.1052884638, -0.05273929295, -0.09804759123, 0.02676341234, 0.0825150306, 0.001318540609, -0.04206423821),
    (-0.0807528844, 0.1433856071, -0.02927536699, -0.1203274859, 0.113532529, 0.04297640002, -0.1359071454, 0.03217281435, 0.1131044363, -0.07497313561, -0.07767707065, 0.08565207726, 0.04832778656, -0.07373331536, -0.0262794175, 0.03977430954),
)
ODD = (
    (-0.06039643671, -0.1619285065, -0.2157655924, -0.2164663713, -0.179285157, -0.1273735765, -0.07932182359, -0.04395383706, -0.0219317145, -0.009956138688, -0.004149848215, -0.001600910605, -0.0005751981407, -0.0001930716936, -6.006259695e-05, -1.532579998e-05),
    (0.06770405989, 0.1570721263, 0.1434280287, 0.04295191184, -0.07879962265, -0.1610074452, -0.1820744199, -0.1564850599, -0.1117106857, -0.06911197019, -0.03803899989, -0.018976138, -0.008700246907, -0.003698004317, -0.001443221181, -0.0004421770918),
    (-0.06672308627, -0.1353009509, -0.07559650806, 0.05145652305, 0.1328476776, 0.1110923906, 0.01620622731, -0.08318512773, -0.1393111579, -0.1451173835, -0.1191406959, -0.08344766078, -0.05189716398, -0.02921471538, -0.01463357191, -0.005358686102),
    (-0.06188570509, -0.1120544487, -0.03164468805, 0.08318098917, 0.1076065769, 0.02554639647, -0.07633334629, -0.1130798134, -0.07076087078, 0.008202589998, 0.07547632887, 0.1077871043, 0.1068753005, 0.08546497618, 0.0555295236, 0.02380489812),
    (0.07294621453, 0.1170272587, 0.0005822684711, -0.1151664239, -0.08239886349, 0.04808258285, 0.1205972232, 0.06802484515, -0.04264531193, -0.1109041826, -0.09690224579, -0.0289313287, 0.0417153054, 0.07952536804, 0.07530043037, 0.03856509779),
    (0.08652145766, 0.1159240548, -0.04433348034, -0.1318825677, -0.0146605442, 0.1210590442, 0.0842447592, -0.05956973628, -0.1239316034, -0.0494564638, 0.06563154857, 0.1089604688, 0.06071412772, -0.01917666675, -0.06207287706, -0.04244003862),
    (0.09796928773, 0.1014768063, -0.091850156, -0.1080980874, 0.07605361357, 0.1198048209, -0.04229231028, -0.1286411677, -0.01461539232, 0.1112662457, 0.07892093947, -0.04457606115, -0.09810478366, -0.03937820657, 0.03879814661, 0.04335854939),
    (0.1083285032, 0.07708721735, -0.1285703026, -0.0450395491, 0.1354076647, 0.02413735124, -0.1328629117, -0.02187888439, 0.1235455303, 0.03873152733, -0.1025408614, -0.0647085451, 0.06221363399, 0.07559191195, -0.01210690766, -0.04280157103),
    (0.1177268554, 0.04504968521, -0.1441555522, 0.03839419971, 0.1212170689, -0.09675550887, -0.07572314606, 0.120135559, 0.03631601591, -0.1190390193, -0.01579049946, 0.1052262271, 0.01219152635, -0.08172301286, -0.01423910674, 0.04104943366),
    (0.126120285, 0.007979130802, -0.1328480522, 0.1116338241, 0.03421605314, -0.1374354291, 0.07279981158, 0.07996744654, -0.1205095327, -0.004441967651, 0.111290914, -0.04516234118, -0.07618300914, 0.05955705328, 0.03710370067, -0.03825468552),
)
EVEN_GAIN = (
    0.7236012542, -0.7236000597, 0.7230899637, -0.6794753044, 0.309908605, -0.04203461377, 0.003110230195, -0.0001597812355, 6.121678833e-06, -1.82449892e-07,
)
ODD_GAIN = (
    0.7236012257, -0.7235710907, 0.7176666509, -0.5402161025, 0.127514432, -0.01205222733, 0.0007337517912, -3.234542573e-05, 1.088270167e-06, -2.894614862e-08,
)
RANK = 10
TURN = 1.0 / (2.0 * math.pi)
SIN_COEFS = (
    6.283182818550517, -41.3414213986335, 81.59618387150637,
    -76.58010050946145, 41.20539479011024, -12.271262230884131,
)
COS_COEFS = (
    0.9999999891722597, -19.739204532088525, 64.93911898360994, -85.45016554540021,
    60.167831693053074, -25.96831316496443, 6.52961023180932,
)
MODE_TILE = 512
OWN_CLASSES = 4
HALO_CLASSES = 8
NT = (((1,), (1,)), ((), ()))
NN = (((1,), (0,)), ((), ()))
BLOCK_AXES = ("x", "z_hi", "y")
MIB = 1024 * 1024


def horner(coefs, square):
    total = jnp.full_like(square, coefs[-1])
    for coef in coefs[-2::-1]:
        total = total * square + coef
    return total


def cos_sin(turns):
    rest = turns - jnp.round(turns)
    square = rest * rest
    return horner(COS_COEFS, square), rest * horner(SIN_COEFS, square)


def dot(a, b, dims=NN):
    return lax.dot_general(a, b, dims, preferred_element_type=jnp.float32)


def split(value):
    high = value.astype(jnp.bfloat16)
    return high, (value - high.astype(jnp.float32)).astype(jnp.bfloat16)


def split3(value):
    high = value.astype(jnp.bfloat16)
    rest = value - high.astype(jnp.float32)
    middle = rest.astype(jnp.bfloat16)
    return high, middle, (rest - middle.astype(jnp.float32)).astype(jnp.bfloat16)


def dot_split(a, b, dims=NN):
    return dot(a[0], b[0], dims) + (dot(a[0], b[1], dims) + dot(a[1], b[0], dims))


def mixing_matrices():
    parts = []
    for matrix, gain in ((EVEN, None), (ODD, None), (EVEN, EVEN_GAIN), (ODD, ODD_GAIN)):
        matrix = np.array(matrix)
        if gain is not None:
            matrix = matrix / np.array(gain)[:, None]
        rest = np.pad(matrix, ((0, 16 - RANK), (0, 0))).astype(np.float32)
        pieces = []
        for _ in range(3):
            pieces.append(rest.astype(jnp.bfloat16))
            rest = rest - pieces[-1].astype(np.float32)
        first, second, third = pieces
        row = np.concatenate([first, first, second, second, first, third], axis=1)
        parts.append(np.pad(row, ((0, 0), (0, 128 - row.shape[1]))))
    return np.concatenate(parts, axis=1).astype(np.float32)


def mix(matrix, value):
    high, middle, low = split3(value)
    return dot(matrix, jnp.concatenate([high, middle, high, middle, low, high], axis=0))


def factors(first, second, mixing):
    width = first.shape[1]
    index = lax.broadcasted_iota(jnp.int32, (16, 1), 0)
    nodes = jnp.zeros((16, 1), jnp.float32)
    for i, node in enumerate(NODES):
        nodes = jnp.where(index == i, node, nodes)
    cos_part, sin_part = cos_sin(nodes * jnp.concatenate([first, second], axis=1))
    evens = mix(mixing[:, :96], cos_part)
    odds = mix(mixing[:, 128:224], sin_part)
    return evens[:, :width], odds[:, :width], evens[:, width:], odds[:, width:]


def outer_rows(left, right):
    for i in range(0, RANK, 2):
        yield jnp.concatenate([left[:8] * right[i : i + 1], left[:8] * right[i + 1 : i + 2]], axis=0)
    for i in range(8, RANK, 2):
        yield jnp.concatenate([left[i : i + 1] * right[:8], left[i + 1 : i + 2] * right[:8]], axis=0)


PAIR_ROWS = 8 * RANK + 8 * (RANK - 8)


def store_rows(high, low, columns, evx, odx, evy, ody, is_cos, sign):
    pairs = ((evx, evy, 1.0), (odx, ody, sign)) if is_cos else ((odx, evy, 1.0), (evx, ody, 1.0))
    row = 0
    for left, right, factor in pairs:
        if factor < 0:
            right = -right
        for value in outer_rows(left, right):
            part = split(value)
            high[row : row + 16, columns] = part[0]
            low[row : row + 16, columns] = part[1]
            row += 16


def as_column(row):
    count = row.shape[1]
    here = lax.broadcasted_iota(jnp.int32, (count, count), 0)
    there = lax.broadcasted_iota(jnp.int32, (count, count), 1)
    return jnp.sum(jnp.where(here == there, row, 0.0), axis=1, keepdims=True)


def structure_kernel(
    sizes, density_far, packed,
    partial, cos_out, sin_out, wave_c_high, wave_c_low, wave_s_high, wave_s_low,
    point_c_high, point_c_low, point_s_high, point_s_low,
    density, form_c, form_s, arrived,
):
    copy = pltpu.make_async_copy(density_far, density, arrived)
    copy.start()
    views, start = [], 0
    for size in sizes:
        padded = -(-size // 128) * 128
        views.append(packed.at[:, start : start + padded])
        start += padded
    waves, points, centers, mixing = views
    mixing = mixing[...].astype(jnp.bfloat16)
    every = slice(None)
    scale = 2.0 * BAND * TURN
    parts = factors(points[0:1, :] * scale, points[1:2, :] * scale, mixing[:, :256])
    store_rows(point_c_high, point_c_low, every, *parts, True, -1.0)
    store_rows(point_s_high, point_s_low, every, *parts, False, 1.0)
    copy.wait()
    dens = density[...]
    held_c = split(dot(dens, point_c_high[...], NT) + dot(dens, point_c_low[...], NT))
    held_s = split(dot(dens, point_s_high[...], NT) + dot(dens, point_s_low[...], NT))
    center_x = as_column(centers[0:1, :][:, : density.shape[0]])
    center_y = as_column(centers[1:2, :][:, : density.shape[0]])
    atoms, modes = cos_out.shape
    tile = min(MODE_TILE, modes)
    for start in range(0, modes, tile):
        here = slice(start, start + tile)
        kx = waves[0:1, here] * TURN
        ky = waves[1:2, here] * TURN
        parts = factors(kx * (BAND / 24.0), ky * (BAND / 24.0), mixing[:, 256:])
        store_rows(wave_c_high, wave_c_low, here, *parts, True, 1.0)
        store_rows(wave_s_high, wave_s_low, here, *parts, False, 1.0)
        form_c[:, here] = dot_split(held_c, (wave_c_high[:, here], wave_c_low[:, here]))
        form_s[:, here] = dot_split(held_s, (wave_s_high[:, here], wave_s_low[:, here]))
        real = jnp.zeros((16, tile), jnp.float32)
        imag = jnp.zeros((16, tile), jnp.float32)
        for row in range(0, atoms, 16):
            rows = slice(row, row + 16)
            cos_c, sin_c = cos_sin(center_x[rows] * kx + center_y[rows] * ky)
            cos_out[rows, here] = cos_c
            sin_out[rows, here] = sin_c
            cos_f, sin_f = form_c[rows, here], form_s[rows, here]
            real = real + (cos_c * cos_f - sin_c * sin_f)
            imag = imag + (sin_c * cos_f + cos_c * sin_f)
        partial[0:1, here] = jnp.sum(real, axis=0, keepdims=True)
        partial[1:2, here] = -jnp.sum(imag, axis=0, keepdims=True)


def partial_structure(density, centers, points, waves):
    atoms, count = density.shape
    modes = waves.shape[1]
    rows = 2 * PAIR_ROWS
    bf16, f32 = jnp.bfloat16, jnp.float32
    mixing = mixing_matrices()
    parts = [waves, points, centers, mixing]
    sizes = [part.shape[1] for part in parts]
    packed = jnp.concatenate(
        [jnp.pad(p, ((0, 16 - p.shape[0]), (0, -p.shape[1] % 128))) for p in parts], axis=1
    )
    out = lambda shape, kind: jax.ShapeDtypeStruct(shape, kind)
    return pl.pallas_call(
        functools.partial(structure_kernel, sizes),
        in_specs=[pl.BlockSpec(memory_space=pltpu.HBM), pl.BlockSpec(memory_space=pltpu.VMEM)],
        out_shape=[out((2, modes), f32)] + [out((atoms, modes), f32)] * 2
        + [out((rows, modes), bf16)] * 4 + [out((rows, count), bf16)] * 4,
        scratch_shapes=[pltpu.VMEM((atoms, count), bf16)]
        + [pltpu.VMEM((atoms, modes), f32)] * 2 + [pltpu.SemaphoreType.DMA],
        compiler_params=pltpu.CompilerParams(vmem_limit_bytes=30 * MIB),
        cost_estimate=pl.CostEstimate(
            flops=16 * atoms * rows * (count * 4 + modes * 6),
            bytes_accessed=8 * atoms * modes, transcendentals=0,
        ),
    )(density, packed)


def far_kernel(
    normalizer, first, second, weight, cos_c, sin_c,
    wave_c_high, wave_c_low, wave_s_high, wave_s_low,
    point_c_high, point_c_low, point_s_high, point_s_low,
    keep, send, spread_c_high, spread_c_low, spread_s_high, spread_s_low, field,
):
    atoms, modes = cos_c.shape
    tile = min(MODE_TILE, modes)
    held_c = held_s = None
    for start in range(0, modes, tile):
        here = slice(start, start + tile)
        scaled = weight[:, here] * normalizer
        real = (first[0:1, here] + second[0:1, here]) * scaled
        imag = (first[1:2, here] + second[1:2, here]) * scaled
        for row in range(0, atoms, 16):
            rows = slice(row, row + 16)
            cosine, sine = cos_c[rows, here], sin_c[rows, here]
            spread_c_high[rows, here], spread_c_low[rows, here] = split(real * cosine - imag * sine)
            spread_s_high[rows, here], spread_s_low[rows, here] = split(-(real * sine + imag * cosine))
        part_c = dot_split(
            (spread_c_high[:, here], spread_c_low[:, here]),
            (wave_c_high[:, here], wave_c_low[:, here]), NT,
        )
        part_s = dot_split(
            (spread_s_high[:, here], spread_s_low[:, here]),
            (wave_s_high[:, here], wave_s_low[:, here]), NT,
        )
        held_c = part_c if held_c is None else held_c + part_c
        held_s = part_s if held_s is None else held_s + part_s
    field[...] = dot_split(
        split(held_c), (point_c_high[...], point_c_low[...])
    ) + dot_split(split(held_s), (point_s_high[...], point_s_low[...]))
    chip, core = lax.axis_index("z_lo"), lax.axis_index("core")
    chips, _, width = keep.shape
    for ahead in range(chips):
        other = jnp.bitwise_xor(chip, ahead)
        mine = pl.multiple_of((2 * other + core) * width, width)
        theirs = pl.multiple_of((2 * other + 1 - core) * width, width)
        keep[ahead] = field[:, pl.ds(mine, width)]
        send[ahead] = field[:, pl.ds(theirs, width)]


def far_partial(normalizer, first, second, weight, cos_c, sin_c, waves, points, chips):
    atoms, modes = cos_c.shape
    rows, count = points[0].shape
    width = count // (2 * chips)
    return pl.pallas_call(
        functools.partial(far_kernel, normalizer),
        out_shape=[jax.ShapeDtypeStruct((chips, atoms, width), jnp.float32)] * 2,
        scratch_shapes=[pltpu.VMEM((atoms, modes), jnp.bfloat16)] * 4
        + [pltpu.VMEM((atoms, count), jnp.float32)],
        compiler_params=pltpu.CompilerParams(vmem_limit_bytes=30 * MIB),
        cost_estimate=pl.CostEstimate(
            flops=2 * atoms * rows * 6 * (count + modes),
            bytes_accessed=8 * atoms * modes, transcendentals=0,
        ),
    )(first, second, weight, cos_c, sin_c, *waves, *points)


def find_places(offsets, atoms_of, counts, atoms):
    classes = offsets.shape[0]
    blocks = lax.axis_size(BLOCK_AXES)
    shift = atoms_of[...] - (lax.axis_index(BLOCK_AXES) - 1) * atoms
    shift = jnp.where(shift < 0, shift + blocks * atoms, shift)
    shift = jnp.where(shift >= blocks * atoms, shift - blocks * atoms, shift)
    live = lax.broadcasted_iota(jnp.int32, shift.shape, 0) < counts[...]
    places = jnp.where(live, shift + 1, 0).astype(jnp.float32)
    of_slot = offsets[...]
    rows = [
        jnp.sum(jnp.where(of_slot == one, places, 0.0), axis=0, keepdims=True)
        for one in range(classes)
    ]
    rows.append(jnp.zeros((-classes % 8, atoms), jnp.float32))
    return jnp.transpose(jnp.concatenate(rows, axis=0))


def near_kernel(group, is_halo, *rest):
    rest, (sources, values, picks, made) = rest[:-4], rest[-4:]
    if is_halo:
        (found, near, start), given, out = rest[:3], rest[3:-1], rest[-1]
    else:
        (offsets, atoms_of, counts, near, start), given = rest[:5], rest[5:-2]
        out, found = rest[-2:]
        found[...] = find_places(offsets, atoms_of, counts, out.shape[0])
    classes, width, count = near.shape
    atoms = out.shape[0]
    used = atoms * len(given)
    wide = picks.shape[2] // group
    for i, block in enumerate(given):
        sources[i * atoms : (i + 1) * atoms, :] = block[...]
    core = lax.axis_index("core")
    column = lax.broadcasted_iota(jnp.int32, (1, wide), 1)
    if is_halo:
        base = jnp.where(column < atoms, core * 2 * atoms, (1 - core) * 2 * atoms - atoms)
    else:
        base = atoms
    target = jnp.where(column < used, column + base + 1, -1).astype(jnp.float32)
    for slot in range(2):
        for one in range(group):
            values[slot, one * wide + used : (one + 1) * wide, :] = jnp.zeros(
                (wide - used, 2 * width), values.dtype
            )
    result = jnp.zeros((atoms, 2 * width), jnp.float32)
    steps = -(-classes // group)
    for step in range(steps + 1):
        slot = step % 2
        size = min(group, classes - step * group)
        before = group if step < steps else classes - (steps - 1) * group
        if step < steps:
            block = near[step * group : step * group + size].reshape(size * width, count)
            made[slot, :, : size * width] = dot(sources[...], block, NT)
            for one in range(size):
                own_class = step * group + one
                chosen = jnp.where(found[:, own_class : own_class + 1] == target, 1.0, 0.0)
                picks[slot, :, one * wide : (one + 1) * wide] = chosen.astype(jnp.bfloat16)
        if step > 0:
            result = result + dot(
                picks[1 - slot, :, : before * wide], values[1 - slot, : before * wide]
            )
        if step < steps:
            for one in range(size):
                high, low = split(made[slot, :, one * width : (one + 1) * width])
                rows = slice(one * wide, one * wide + used)
                values[slot, rows, :width] = high
                values[slot, rows, width:] = low
    if is_halo:
        begin = start[...]
    else:
        member = lax.axis_index("z_lo") * 2 + core
        mine = pl.multiple_of(member * width, width)
        begin = 0.5 * start[:, pl.ds(mine, width)].astype(jnp.float32)
    out[...] = begin + (result[:, :width] + result[:, width:])


def near_part(is_halo, lists, near, start, given):
    atoms = given[0].shape[0]
    classes, width, count = near.shape
    group = min(HALO_CLASSES if is_halo else OWN_CLASSES, classes)
    used = atoms * len(given)
    wide = -(-used // 128) * 128
    bf16, f32 = jnp.bfloat16, jnp.float32
    out = jax.ShapeDtypeStruct((atoms, width), f32)
    found = jax.ShapeDtypeStruct((atoms, -(-classes // 8) * 8), f32)
    return pl.pallas_call(
        functools.partial(near_kernel, group, is_halo),
        scratch_shapes=[
            pltpu.VMEM((used, count), bf16), pltpu.VMEM((2, group * wide, 2 * width), bf16),
            pltpu.VMEM((2, atoms, group * wide), bf16), pltpu.VMEM((2, used, group * width), f32),
        ],
        out_shape=out if is_halo else [out, found],
        compiler_params=pltpu.CompilerParams(vmem_limit_bytes=30 * MIB),
        cost_estimate=pl.CostEstimate(
            flops=2 * used * classes * width * (count + 2 * atoms),
            bytes_accessed=2 * classes * width * count, transcendentals=0,
        ),
    )(*lists, near, start, *given)


def fold_kernel(keep, taken, *outs):
    for ahead, out in enumerate(outs):
        out[...] = keep[ahead] + taken[ahead]


def fold(keep, taken):
    chips, atoms, width = keep.shape
    return pl.pallas_call(
        fold_kernel,
        out_shape=[jax.ShapeDtypeStruct((atoms, width), jnp.float32)] * chips,
        compiler_params=pltpu.CompilerParams(vmem_limit_bytes=8 * MIB),
    )(keep, taken)


def shifted(value, axis, by):
    count = lax.axis_size(axis)
    return lax.ppermute(value, axis, [(i, (i + by) % count) for i in range(count)])


def sum_over(value, axis):
    count = lax.axis_size(axis)
    return value + sum(shifted(value, axis, by) for by in range(1, count))


def shards(
    density, near_blocks, neighbour_atoms, neighbour_offsets, neighbour_counts,
    centers, local_points, wavevectors, spectral_weight,
):
    atoms, points = density.shape
    blocks = lax.axis_size(BLOCK_AXES)
    modes = wavevectors.shape[1]
    chips, cores = lax.axis_size("z_lo"), lax.axis_size("core")
    normalizer = 1.0 / math.sqrt(atoms * blocks * points * modes * chips * cores)

    halo_route = []
    ring = lax.axis_size("y")
    for source in range(blocks):
        for chip in range(chips):
            for core, target in ((0, (source + 1) % blocks), (1, (source - 1) % blocks)):
                to = chip if source // ring == target // ring else (chip + chips // 2) % chips
                halo_route.append(((source * chips + chip) * 2 + core, (target * chips + to) * 2 + core))
    halo = lax.ppermute(density, BLOCK_AXES + ("z_lo", "core"), halo_route)

    partial, cos_c, sin_c, *tables = partial_structure(density, centers, local_points, wavevectors)

    lists = (neighbour_offsets.T, neighbour_atoms.T, neighbour_counts[None, :])
    near_own, found = near_part(False, lists, near_blocks, density, [density])

    structure = sum_over(partial, "y")
    structure = sum_over(structure, "x")
    other_half = shifted(structure, "z_hi", 1)
    halo_other = lax.ppermute(halo, "core", [(0, 1), (1, 0)])

    structure, near_own = lax.optimization_barrier((structure, near_own))
    keep, send = far_partial(
        normalizer, structure, other_half, spectral_weight[None, :], cos_c, sin_c,
        tables[:4], tables[4:], chips,
    )
    taken = lax.ppermute(send, "core", [(0, 1), (1, 0)])
    near_field = near_part(True, [found], near_blocks, near_own, [halo, halo_other])
    far_field = keep[0] + taken[0]
    for by in range(chips - 1, 0, -1):
        swap = [(i, i ^ by) for i in range(chips)]
        piece = ((keep[by] + taken[by]) * (1.0 / 32.0)).astype(jnp.float16)
        far_field = far_field + lax.ppermute(piece, "z_lo", swap).astype(jnp.float32) * 32.0
    return near_field + far_field


def solution(mesh):
    fine = Mesh(
        mesh.devices.reshape(4, 2, 4, 4, 2), ("x", "z_hi", "y", "z_lo", "core")
    )
    modes = ("z_lo", "core")
    placed = (
        P(BLOCK_AXES, None), P(None, modes, None), P(BLOCK_AXES, None), P(BLOCK_AXES, None),
        P(BLOCK_AXES), P(None, BLOCK_AXES), P(), P(None, modes), P(modes),
    )
    return jax.shard_map(
        shards, mesh=fine, in_specs=placed, out_specs=P(BLOCK_AXES, modes), check_vma=False
    )
```

```python
import functools
import math

import jax
import jax.numpy as jnp
import numpy as np
from jax import lax
from jax.experimental import pallas as pl
from jax.experimental.pallas import tpu as pltpu
from jax.sharding import Mesh
from jax.sharding import PartitionSpec as P

BAND = 12.0
NODES = (
    0.04830766569, 0.1444719616, 0.2392873623, 0.3318686023, 0.4213512761, 0.5068999089, 0.5877157572, 0.6630442669, 0.7321821187, 0.794483796, 0.8493676137, 0.8963211558, 0.9349060759, 0.9647622556, 0.9856115115, 0.9972638618,
)
EVEN = (
    (0.264161544, 0.235683413, 0.1877892764, 0.1338856267, 0.08565638585, 0.04935936307, 0.02573553405, 0.01220462496, 0.005294905203, 0.00211445586, 0.0007820202318, 0.0002693802975, 8.679038294e-05, 2.6181341e-05, 7.331099629e-06, 1.708479253e-06),
    (0.1702613529, 0.08465650818, -0.04082940747, -0.1469360259, -0.1970030198, -0.1901061112, -0.1489564192, -0.09954602317, -0.05833865755, -0.03055765255, -0.01451635874, -0.006328267813, -0.002555179594, -0.0009609245647, -0.000333851875, -9.333966862e-05),
    (-0.1323973182, -0.02247601982, 0.1047497372, 0.1503633392, 0.08986991162, -0.02455938248, -0.1219371619, -0.1640572477, -0.1545048367, -0.1178161583, -0.07717100148, -0.0448976056, -0.02371842969, -0.01152257368, -0.005081924909, -0.001704677766),
    (-0.1038663831, 0.008772611212, 0.1112611228, 0.09900945939, -0.007887275225, -0.1049440761, -0.1157944762, -0.04697227583, 0.04443730952, 0.108316557, 0.1285622126, 0.1155652092, 0.08749662772, 0.05797221816, 0.03303595529, 0.01312861586),
    (-0.09524794649, 0.02681958951, 0.1142235556, 0.06137473355, -0.06159895528, -0.114537939, -0.05174444256, 0.05425346059, 0.1112188114, 0.08907465173, 0.01933187924, -0.05021028773, -0.08987667008, -0.09410761546, -0.0713193742, -0.03310624913),
    (0.1022051591, -0.05281704117, -0.1277713562, -0.0158252522, 0.116158395, 0.09060969529, -0.0463884297, -0.1239497875, -0.06822339825, 0.04641750905, 0.1115635062, 0.08861974282, 0.01440006111, -0.05133346873, -0.07076867034, -0.04114204128),
    (-0.1016349432, 0.081731359, 0.1180899649, -0.05213972209, -0.1310463958, 0.004828729775, 0.1285200703, 0.06026154641, -0.08513107212, -0.1134175056, -0.009982527353, 0.09053034847, 0.0894231339, 0.01200695961, -0.051135621, -0.04311496388),
    (-0.09691907606, 0.1086033655, 0.08463923718, -0.1138806091, -0.07938954229, 0.1091864505, 0.0866221684, -0.08980194788, -0.1037585862, 0.04854215716, 0.1134990489, 0.01271606801, -0.08781269714, -0.0609974537, 0.02562700126, 0.04324151356),
    (-0.08972912127, 0.1300425509, 0.03237330507, -0.1418919531, 0.02055363161, 0.132001602, -0.05367707241, -0.1161966312, 0.06348478865, 0.1052884638, -0.05273929295, -0.09804759123, 0.02676341234, 0.0825150306, 0.001318540609, -0.04206423821),
    (-0.0807528844, 0.1433856071, -0.02927536699, -0.1203274859, 0.113532529, 0.04297640002, -0.1359071454, 0.03217281435, 0.1131044363, -0.07497313561, -0.07767707065, 0.08565207726, 0.04832778656, -0.07373331536, -0.0262794175, 0.03977430954),
)
ODD = (
    (-0.06039643671, -0.1619285065, -0.2157655924, -0.2164663713, -0.179285157, -0.1273735765, -0.07932182359, -0.04395383706, -0.0219317145, -0.009956138688, -0.004149848215, -0.001600910605, -0.0005751981407, -0.0001930716936, -6.006259695e-05, -1.532579998e-05),
    (0.06770405989, 0.1570721263, 0.1434280287, 0.04295191184, -0.07879962265, -0.1610074452, -0.1820744199, -0.1564850599, -0.1117106857, -0.06911197019, -0.03803899989, -0.018976138, -0.008700246907, -0.003698004317, -0.001443221181, -0.0004421770918),
    (-0.06672308627, -0.1353009509, -0.07559650806, 0.05145652305, 0.1328476776, 0.1110923906, 0.01620622731, -0.08318512773, -0.1393111579, -0.1451173835, -0.1191406959, -0.08344766078, -0.05189716398, -0.02921471538, -0.01463357191, -0.005358686102),
    (-0.06188570509, -0.1120544487, -0.03164468805, 0.08318098917, 0.1076065769, 0.02554639647, -0.07633334629, -0.1130798134, -0.07076087078, 0.008202589998, 0.07547632887, 0.1077871043, 0.1068753005, 0.08546497618, 0.0555295236, 0.02380489812),
    (0.07294621453, 0.1170272587, 0.0005822684711, -0.1151664239, -0.08239886349, 0.04808258285, 0.1205972232, 0.06802484515, -0.04264531193, -0.1109041826, -0.09690224579, -0.0289313287, 0.0417153054, 0.07952536804, 0.07530043037, 0.03856509779),
    (0.08652145766, 0.1159240548, -0.04433348034, -0.1318825677, -0.0146605442, 0.1210590442, 0.0842447592, -0.05956973628, -0.1239316034, -0.0494564638, 0.06563154857, 0.1089604688, 0.06071412772, -0.01917666675, -0.06207287706, -0.04244003862),
    (0.09796928773, 0.1014768063, -0.091850156, -0.1080980874, 0.07605361357, 0.1198048209, -0.04229231028, -0.1286411677, -0.01461539232, 0.1112662457, 0.07892093947, -0.04457606115, -0.09810478366, -0.03937820657, 0.03879814661, 0.04335854939),
    (0.1083285032, 0.07708721735, -0.1285703026, -0.0450395491, 0.1354076647, 0.02413735124, -0.1328629117, -0.02187888439, 0.1235455303, 0.03873152733, -0.1025408614, -0.0647085451, 0.06221363399, 0.07559191195, -0.01210690766, -0.04280157103),
    (0.1177268554, 0.04504968521, -0.1441555522, 0.03839419971, 0.1212170689, -0.09675550887, -0.07572314606, 0.120135559, 0.03631601591, -0.1190390193, -0.01579049946, 0.1052262271, 0.01219152635, -0.08172301286, -0.01423910674, 0.04104943366),
    (0.126120285, 0.007979130802, -0.1328480522, 0.1116338241, 0.03421605314, -0.1374354291, 0.07279981158, 0.07996744654, -0.1205095327, -0.004441967651, 0.111290914, -0.04516234118, -0.07618300914, 0.05955705328, 0.03710370067, -0.03825468552),
)
EVEN_GAIN = (
    0.7236012542, -0.7236000597, 0.7230899637, -0.6794753044, 0.309908605, -0.04203461377, 0.003110230195, -0.0001597812355, 6.121678833e-06, -1.82449892e-07,
)
ODD_GAIN = (
    0.7236012257, -0.7235710907, 0.7176666509, -0.5402161025, 0.127514432, -0.01205222733, 0.0007337517912, -3.234542573e-05, 1.088270167e-06, -2.894614862e-08,
)
RANK = 10
TURN = 1.0 / (2.0 * math.pi)
SIN_COEFS = (
    6.283182818550517, -41.3414213986335, 81.59618387150637,
    -76.58010050946145, 41.20539479011024, -12.271262230884131,
)
COS_COEFS = (
    0.9999999891722597, -19.739204532088525, 64.93911898360994, -85.45016554540021,
    60.167831693053074, -25.96831316496443, 6.52961023180932,
)
MODE_TILE = 512
OWN_CLASSES = 4
HALO_CLASSES = 8
NT = (((1,), (1,)), ((), ()))
NN = (((1,), (0,)), ((), ()))
BLOCK_AXES = ("x", "z_hi", "y")
MIB = 1024 * 1024


def horner(coefs, square):
    total = jnp.full_like(square, coefs[-1])
    for coef in coefs[-2::-1]:
        total = total * square + coef
    return total


def cos_sin(turns):
    rest = turns - jnp.round(turns)
    square = rest * rest
    return horner(COS_COEFS, square), rest * horner(SIN_COEFS, square)


def dot(a, b, dims=NN):
    return lax.dot_general(a, b, dims, preferred_element_type=jnp.float32)


def split(value):
    high = value.astype(jnp.bfloat16)
    return high, (value - high.astype(jnp.float32)).astype(jnp.bfloat16)


def split3(value):
    high = value.astype(jnp.bfloat16)
    rest = value - high.astype(jnp.float32)
    middle = rest.astype(jnp.bfloat16)
    return high, middle, (rest - middle.astype(jnp.float32)).astype(jnp.bfloat16)


def dot_split(a, b, dims=NN):
    return dot(a[0], b[0], dims) + (dot(a[0], b[1], dims) + dot(a[1], b[0], dims))


def mixing_matrices():
    parts = []
    for matrix, gain in ((EVEN, None), (ODD, None), (EVEN, EVEN_GAIN), (ODD, ODD_GAIN)):
        matrix = np.array(matrix)
        if gain is not None:
            matrix = matrix / np.array(gain)[:, None]
        rest = np.pad(matrix, ((0, 16 - RANK), (0, 0))).astype(np.float32)
        pieces = []
        for _ in range(3):
            pieces.append(rest.astype(jnp.bfloat16))
            rest = rest - pieces[-1].astype(np.float32)
        first, second, third = pieces
        row = np.concatenate([first, first, second, second, first, third], axis=1)
        parts.append(np.pad(row, ((0, 0), (0, 128 - row.shape[1]))))
    return np.concatenate(parts, axis=1).astype(np.float32)


def mix(matrix, value):
    high, middle, low = split3(value)
    return dot(matrix, jnp.concatenate([high, middle, high, middle, low, high], axis=0))


def factors(first, second, mixing):
    width = first.shape[1]
    index = lax.broadcasted_iota(jnp.int32, (16, 1), 0)
    nodes = jnp.zeros((16, 1), jnp.float32)
    for i, node in enumerate(NODES):
        nodes = jnp.where(index == i, node, nodes)
    cos_part, sin_part = cos_sin(nodes * jnp.concatenate([first, second], axis=1))
    evens = mix(mixing[:, :96], cos_part)
    odds = mix(mixing[:, 128:224], sin_part)
    return evens[:, :width], odds[:, :width], evens[:, width:], odds[:, width:]


def outer_rows(left, right):
    for i in range(0, RANK, 2):
        yield jnp.concatenate([left[:8] * right[i : i + 1], left[:8] * right[i + 1 : i + 2]], axis=0)
    for i in range(8, RANK, 2):
        yield jnp.concatenate([left[i : i + 1] * right[:8], left[i + 1 : i + 2] * right[:8]], axis=0)


PAIR_ROWS = 8 * RANK + 8 * (RANK - 8)


def store_rows(high, low, columns, evx, odx, evy, ody, is_cos, sign):
    pairs = ((evx, evy, 1.0), (odx, ody, sign)) if is_cos else ((odx, evy, 1.0), (evx, ody, 1.0))
    row = 0
    for left, right, factor in pairs:
        if factor < 0:
            right = -right
        for value in outer_rows(left, right):
            part = split(value)
            high[row : row + 16, columns] = part[0]
            low[row : row + 16, columns] = part[1]
            row += 16


def as_column(row):
    count = row.shape[1]
    here = lax.broadcasted_iota(jnp.int32, (count, count), 0)
    there = lax.broadcasted_iota(jnp.int32, (count, count), 1)
    return jnp.sum(jnp.where(here == there, row, 0.0), axis=1, keepdims=True)


def structure_kernel(
    sizes, density_far, packed,
    density, partial, cos_out, sin_out, wave_c_high, wave_c_low, wave_s_high, wave_s_low,
    point_c_high, point_c_low, point_s_high, point_s_low,
    form_c, form_s, arrived,
):
    copy = pltpu.make_async_copy(density_far, density, arrived)
    copy.start()
    views, start = [], 0
    for size in sizes:
        padded = -(-size // 128) * 128
        views.append(packed.at[:, start : start + padded])
        start += padded
    waves, points, centers, mixing = views
    mixing = mixing[...].astype(jnp.bfloat16)
    every = slice(None)
    scale = 2.0 * BAND * TURN
    parts = factors(points[0:1, :] * scale, points[1:2, :] * scale, mixing[:, :256])
    store_rows(point_c_high, point_c_low, every, *parts, True, -1.0)
    store_rows(point_s_high, point_s_low, every, *parts, False, 1.0)
    copy.wait()
    dens = density[...]
    held_c = split(dot(dens, point_c_high[...], NT) + dot(dens, point_c_low[...], NT))
    held_s = split(dot(dens, point_s_high[...], NT) + dot(dens, point_s_low[...], NT))
    center_x = as_column(centers[0:1, :][:, : density.shape[0]])
    center_y = as_column(centers[1:2, :][:, : density.shape[0]])
    atoms, modes = cos_out.shape
    tile = min(MODE_TILE, modes)
    for start in range(0, modes, tile):
        here = slice(start, start + tile)
        kx = waves[0:1, here] * TURN
        ky = waves[1:2, here] * TURN
        parts = factors(kx * (BAND / 24.0), ky * (BAND / 24.0), mixing[:, 256:])
        store_rows(wave_c_high, wave_c_low, here, *parts, True, 1.0)
        store_rows(wave_s_high, wave_s_low, here, *parts, False, 1.0)
        form_c[:, here] = dot_split(held_c, (wave_c_high[:, here], wave_c_low[:, here]))
        form_s[:, here] = dot_split(held_s, (wave_s_high[:, here], wave_s_low[:, here]))
        real = jnp.zeros((16, tile), jnp.float32)
        imag = jnp.zeros((16, tile), jnp.float32)
        for row in range(0, atoms, 16):
            rows = slice(row, row + 16)
            cos_c, sin_c = cos_sin(center_x[rows] * kx + center_y[rows] * ky)
            cos_out[rows, here] = cos_c
            sin_out[rows, here] = sin_c
            cos_f, sin_f = form_c[rows, here], form_s[rows, here]
            real = real + (cos_c * cos_f - sin_c * sin_f)
            imag = imag + (sin_c * cos_f + cos_c * sin_f)
        partial[0:1, here] = jnp.sum(real, axis=0, keepdims=True)
        partial[1:2, here] = -jnp.sum(imag, axis=0, keepdims=True)


def partial_structure(density, centers, points, waves):
    atoms, count = density.shape
    modes = waves.shape[1]
    rows = 2 * PAIR_ROWS
    bf16, f32 = jnp.bfloat16, jnp.float32
    mixing = mixing_matrices()
    parts = [waves, points, centers, mixing]
    sizes = [part.shape[1] for part in parts]
    packed = jnp.concatenate(
        [jnp.pad(p, ((0, 16 - p.shape[0]), (0, -p.shape[1] % 128))) for p in parts], axis=1
    )
    out = lambda shape, kind: jax.ShapeDtypeStruct(shape, kind)
    return pl.pallas_call(
        functools.partial(structure_kernel, sizes),
        in_specs=[pl.BlockSpec(memory_space=pltpu.HBM), pl.BlockSpec(memory_space=pltpu.VMEM)],
        out_shape=[out((atoms, count), bf16), out((2, modes), f32)] + [out((atoms, modes), f32)] * 2
        + [out((rows, modes), bf16)] * 4 + [out((rows, count), bf16)] * 4,
        scratch_shapes=[pltpu.VMEM((atoms, modes), f32)] * 2 + [pltpu.SemaphoreType.DMA],
        compiler_params=pltpu.CompilerParams(vmem_limit_bytes=30 * MIB),
        cost_estimate=pl.CostEstimate(
            flops=16 * atoms * rows * (count * 4 + modes * 6),
            bytes_accessed=8 * atoms * modes, transcendentals=0,
        ),
    )(density, packed)


def far_kernel(
    normalizer, first, second, weight, cos_c, sin_c,
    wave_c_high, wave_c_low, wave_s_high, wave_s_low,
    point_c_high, point_c_low, point_s_high, point_s_low,
    keep, send, spread_c_high, spread_c_low, spread_s_high, spread_s_low, field,
):
    atoms, modes = cos_c.shape
    tile = min(MODE_TILE, modes)
    held_c = held_s = None
    for start in range(0, modes, tile):
        here = slice(start, start + tile)
        scaled = weight[:, here] * normalizer
        real = (first[0:1, here] + second[0:1, here]) * scaled
        imag = (first[1:2, here] + second[1:2, here]) * scaled
        for row in range(0, atoms, 16):
            rows = slice(row, row + 16)
            cosine, sine = cos_c[rows, here], sin_c[rows, here]
            spread_c_high[rows, here], spread_c_low[rows, here] = split(real * cosine - imag * sine)
            spread_s_high[rows, here], spread_s_low[rows, here] = split(-(real * sine + imag * cosine))
        part_c = dot_split(
            (spread_c_high[:, here], spread_c_low[:, here]),
            (wave_c_high[:, here], wave_c_low[:, here]), NT,
        )
        part_s = dot_split(
            (spread_s_high[:, here], spread_s_low[:, here]),
            (wave_s_high[:, here], wave_s_low[:, here]), NT,
        )
        held_c = part_c if held_c is None else held_c + part_c
        held_s = part_s if held_s is None else held_s + part_s
    field[...] = dot_split(
        split(held_c), (point_c_high[...], point_c_low[...])
    ) + dot_split(split(held_s), (point_s_high[...], point_s_low[...]))
    chip, core = lax.axis_index("z_lo"), lax.axis_index("core")
    chips, _, width = keep.shape
    for ahead in range(chips):
        other = jnp.bitwise_xor(chip, ahead)
        mine = pl.multiple_of((2 * other + core) * width, width)
        theirs = pl.multiple_of((2 * other + 1 - core) * width, width)
        keep[ahead] = field[:, pl.ds(mine, width)]
        send[ahead] = field[:, pl.ds(theirs, width)]


def far_partial(normalizer, first, second, weight, cos_c, sin_c, waves, points, chips):
    atoms, modes = cos_c.shape
    rows, count = points[0].shape
    width = count // (2 * chips)
    return pl.pallas_call(
        functools.partial(far_kernel, normalizer),
        out_shape=[jax.ShapeDtypeStruct((chips, atoms, width), jnp.float32)] * 2,
        scratch_shapes=[pltpu.VMEM((atoms, modes), jnp.bfloat16)] * 4
        + [pltpu.VMEM((atoms, count), jnp.float32)],
        compiler_params=pltpu.CompilerParams(vmem_limit_bytes=30 * MIB),
        cost_estimate=pl.CostEstimate(
            flops=2 * atoms * rows * 6 * (count + modes),
            bytes_accessed=8 * atoms * modes, transcendentals=0,
        ),
    )(first, second, weight, cos_c, sin_c, *waves, *points)


def find_places(offsets, atoms_of, counts, atoms):
    classes = offsets.shape[0]
    blocks = lax.axis_size(BLOCK_AXES)
    shift = atoms_of[...] - (lax.axis_index(BLOCK_AXES) - 1) * atoms
    shift = jnp.where(shift < 0, shift + blocks * atoms, shift)
    shift = jnp.where(shift >= blocks * atoms, shift - blocks * atoms, shift)
    live = lax.broadcasted_iota(jnp.int32, shift.shape, 0) < counts[...]
    places = jnp.where(live, shift + 1, 0).astype(jnp.float32)
    of_slot = offsets[...]
    rows = [
        jnp.sum(jnp.where(of_slot == one, places, 0.0), axis=0, keepdims=True)
        for one in range(classes)
    ]
    rows.append(jnp.zeros((-classes % 8, atoms), jnp.float32))
    return jnp.transpose(jnp.concatenate(rows, axis=0))


def near_kernel(group, is_halo, *rest):
    rest, (sources, values, picks, made) = rest[:-4], rest[-4:]
    if is_halo:
        (found, near, start), given, out = rest[:3], rest[3:-1], rest[-1]
    else:
        (offsets, atoms_of, counts, near), given = rest[:4], rest[4:-2]
        out, found = rest[-2:]
        found[...] = find_places(offsets, atoms_of, counts, out.shape[0])
    classes, width, count = near.shape
    atoms = out.shape[0]
    used = atoms * len(given)
    wide = picks.shape[2] // group
    for i, block in enumerate(given):
        sources[i * atoms : (i + 1) * atoms, :] = block[...]
    core = lax.axis_index("core")
    column = lax.broadcasted_iota(jnp.int32, (1, wide), 1)
    if is_halo:
        base = jnp.where(column < atoms, core * 2 * atoms, (1 - core) * 2 * atoms - atoms)
    else:
        base = atoms
    target = jnp.where(column < used, column + base + 1, -1).astype(jnp.float32)
    for slot in range(2):
        for one in range(group):
            values[slot, one * wide + used : (one + 1) * wide, :] = jnp.zeros(
                (wide - used, 2 * width), values.dtype
            )
    result = jnp.zeros((atoms, 2 * width), jnp.float32)
    steps = -(-classes // group)
    for step in range(steps + 1):
        slot = step % 2
        size = min(group, classes - step * group)
        before = group if step < steps else classes - (steps - 1) * group
        if step < steps:
            block = near[step * group : step * group + size].reshape(size * width, count)
            made[slot, :, : size * width] = dot(sources[...], block, NT)
            for one in range(size):
                own_class = step * group + one
                chosen = jnp.where(found[:, own_class : own_class + 1] == target, 1.0, 0.0)
                picks[slot, :, one * wide : (one + 1) * wide] = chosen.astype(jnp.bfloat16)
        if step > 0:
            result = result + dot(
                picks[1 - slot, :, : before * wide], values[1 - slot, : before * wide]
            )
        if step < steps:
            for one in range(size):
                high, low = split(made[slot, :, one * width : (one + 1) * width])
                rows = slice(one * wide, one * wide + used)
                values[slot, rows, :width] = high
                values[slot, rows, width:] = low
    if is_halo:
        begin = start[...]
    else:
        member = lax.axis_index("z_lo") * 2 + core
        mine = pl.multiple_of(member * width, width)
        begin = 0.5 * given[0][:, pl.ds(mine, width)].astype(jnp.float32)
    out[...] = begin + (result[:, :width] + result[:, width:])


def near_part(is_halo, lists, near, start, given):
    atoms = given[0].shape[0]
    classes, width, count = near.shape
    group = min(HALO_CLASSES if is_halo else OWN_CLASSES, classes)
    used = atoms * len(given)
    wide = -(-used // 128) * 128
    bf16, f32 = jnp.bfloat16, jnp.float32
    out = jax.ShapeDtypeStruct((atoms, width), f32)
    found = jax.ShapeDtypeStruct((atoms, -(-classes // 8) * 8), f32)
    return pl.pallas_call(
        functools.partial(near_kernel, group, is_halo),
        scratch_shapes=[
            pltpu.VMEM((used, count), bf16), pltpu.VMEM((2, group * wide, 2 * width), bf16),
            pltpu.VMEM((2, atoms, group * wide), bf16), pltpu.VMEM((2, used, group * width), f32),
        ],
        out_shape=out if is_halo else [out, found],
        compiler_params=pltpu.CompilerParams(vmem_limit_bytes=30 * MIB),
        cost_estimate=pl.CostEstimate(
            flops=2 * used * classes * width * (count + 2 * atoms),
            bytes_accessed=2 * classes * width * count, transcendentals=0,
        ),
    )(*lists, near, *start, *given)


def fold_kernel(keep, taken, *outs):
    for ahead, out in enumerate(outs):
        out[...] = keep[ahead] + taken[ahead]


def fold(keep, taken):
    chips, atoms, width = keep.shape
    return pl.pallas_call(
        fold_kernel,
        out_shape=[jax.ShapeDtypeStruct((atoms, width), jnp.float32)] * chips,
        compiler_params=pltpu.CompilerParams(vmem_limit_bytes=8 * MIB),
    )(keep, taken)


def shifted(value, axis, by):
    count = lax.axis_size(axis)
    return lax.ppermute(value, axis, [(i, (i + by) % count) for i in range(count)])


def sum_over(value, axis):
    count = lax.axis_size(axis)
    return value + sum(shifted(value, axis, by) for by in range(1, count))


def shards(
    density, near_blocks, neighbour_atoms, neighbour_offsets, neighbour_counts,
    centers, local_points, wavevectors, spectral_weight,
):
    atoms, points = density.shape
    blocks = lax.axis_size(BLOCK_AXES)
    modes = wavevectors.shape[1]
    chips, cores = lax.axis_size("z_lo"), lax.axis_size("core")
    normalizer = 1.0 / math.sqrt(atoms * blocks * points * modes * chips * cores)

    halo_route = []
    ring = lax.axis_size("y")
    for source in range(blocks):
        for chip in range(chips):
            for core, target in ((0, (source + 1) % blocks), (1, (source - 1) % blocks)):
                to = chip if source // ring == target // ring else (chip + chips // 2) % chips
                halo_route.append(((source * chips + chip) * 2 + core, (target * chips + to) * 2 + core))
    halo = lax.ppermute(density, BLOCK_AXES + ("z_lo", "core"), halo_route)

    own, partial, cos_c, sin_c, *tables = partial_structure(density, centers, local_points, wavevectors)

    lists = (neighbour_offsets.T, neighbour_atoms.T, neighbour_counts[None, :])
    near_own, found = near_part(False, lists, near_blocks, [], [own])

    structure = sum_over(partial, "y")
    structure = sum_over(structure, "x")
    other_half = shifted(structure, "z_hi", 1)
    halo_other = lax.ppermute(halo, "core", [(0, 1), (1, 0)])

    structure, near_own = lax.optimization_barrier((structure, near_own))
    keep, send = far_partial(
        normalizer, structure, other_half, spectral_weight[None, :], cos_c, sin_c,
        tables[:4], tables[4:], chips,
    )
    taken = lax.ppermute(send, "core", [(0, 1), (1, 0)])
    near_field = near_part(True, [found], near_blocks, [near_own], [halo, halo_other])
    far_field = keep[0] + taken[0]
    for by in range(chips - 1, 0, -1):
        swap = [(i, i ^ by) for i in range(chips)]
        piece = ((keep[by] + taken[by]) * (1.0 / 32.0)).astype(jnp.float16)
        far_field = far_field + lax.ppermute(piece, "z_lo", swap).astype(jnp.float32) * 32.0
    return near_field + far_field


def solution(mesh):
    fine = Mesh(
        mesh.devices.reshape(4, 2, 4, 4, 2), ("x", "z_hi", "y", "z_lo", "core")
    )
    modes = ("z_lo", "core")
    placed = (
        P(BLOCK_AXES, None), P(None, modes, None), P(BLOCK_AXES, None), P(BLOCK_AXES, None),
        P(BLOCK_AXES), P(None, BLOCK_AXES), P(), P(None, modes), P(modes),
    )
    return jax.shard_map(
        shards, mesh=fine, in_specs=placed, out_specs=P(BLOCK_AXES, modes), check_vma=False
    )
```

```python
import functools
import math

import jax
import jax.numpy as jnp
import numpy as np
from jax import lax
from jax.experimental import pallas as pl
from jax.experimental.pallas import tpu as pltpu
from jax.sharding import Mesh
from jax.sharding import PartitionSpec as P

BAND = 12.0
NODES = (
    0.04830766569, 0.1444719616, 0.2392873623, 0.3318686023, 0.4213512761, 0.5068999089, 0.5877157572, 0.6630442669, 0.7321821187, 0.794483796, 0.8493676137, 0.8963211558, 0.9349060759, 0.9647622556, 0.9856115115, 0.9972638618,
)
EVEN = (
    (0.264161544, 0.235683413, 0.1877892764, 0.1338856267, 0.08565638585, 0.04935936307, 0.02573553405, 0.01220462496, 0.005294905203, 0.00211445586, 0.0007820202318, 0.0002693802975, 8.679038294e-05, 2.6181341e-05, 7.331099629e-06, 1.708479253e-06),
    (0.1702613529, 0.08465650818, -0.04082940747, -0.1469360259, -0.1970030198, -0.1901061112, -0.1489564192, -0.09954602317, -0.05833865755, -0.03055765255, -0.01451635874, -0.006328267813, -0.002555179594, -0.0009609245647, -0.000333851875, -9.333966862e-05),
    (-0.1323973182, -0.02247601982, 0.1047497372, 0.1503633392, 0.08986991162, -0.02455938248, -0.1219371619, -0.1640572477, -0.1545048367, -0.1178161583, -0.07717100148, -0.0448976056, -0.02371842969, -0.01152257368, -0.005081924909, -0.001704677766),
    (-0.1038663831, 0.008772611212, 0.1112611228, 0.09900945939, -0.007887275225, -0.1049440761, -0.1157944762, -0.04697227583, 0.04443730952, 0.108316557, 0.1285622126, 0.1155652092, 0.08749662772, 0.05797221816, 0.03303595529, 0.01312861586),
    (-0.09524794649, 0.02681958951, 0.1142235556, 0.06137473355, -0.06159895528, -0.114537939, -0.05174444256, 0.05425346059, 0.1112188114, 0.08907465173, 0.01933187924, -0.05021028773, -0.08987667008, -0.09410761546, -0.0713193742, -0.03310624913),
    (0.1022051591, -0.05281704117, -0.1277713562, -0.0158252522, 0.116158395, 0.09060969529, -0.0463884297, -0.1239497875, -0.06822339825, 0.04641750905, 0.1115635062, 0.08861974282, 0.01440006111, -0.05133346873, -0.07076867034, -0.04114204128),
    (-0.1016349432, 0.081731359, 0.1180899649, -0.05213972209, -0.1310463958, 0.004828729775, 0.1285200703, 0.06026154641, -0.08513107212, -0.1134175056, -0.009982527353, 0.09053034847, 0.0894231339, 0.01200695961, -0.051135621, -0.04311496388),
    (-0.09691907606, 0.1086033655, 0.08463923718, -0.1138806091, -0.07938954229, 0.1091864505, 0.0866221684, -0.08980194788, -0.1037585862, 0.04854215716, 0.1134990489, 0.01271606801, -0.08781269714, -0.0609974537, 0.02562700126, 0.04324151356),
    (-0.08972912127, 0.1300425509, 0.03237330507, -0.1418919531, 0.02055363161, 0.132001602, -0.05367707241, -0.1161966312, 0.06348478865, 0.1052884638, -0.05273929295, -0.09804759123, 0.02676341234, 0.0825150306, 0.001318540609, -0.04206423821),
    (-0.0807528844, 0.1433856071, -0.02927536699, -0.1203274859, 0.113532529, 0.04297640002, -0.1359071454, 0.03217281435, 0.1131044363, -0.07497313561, -0.07767707065, 0.08565207726, 0.04832778656, -0.07373331536, -0.0262794175, 0.03977430954),
)
ODD = (
    (-0.06039643671, -0.1619285065, -0.2157655924, -0.2164663713, -0.179285157, -0.1273735765, -0.07932182359, -0.04395383706, -0.0219317145, -0.009956138688, -0.004149848215, -0.001600910605, -0.0005751981407, -0.0001930716936, -6.006259695e-05, -1.532579998e-05),
    (0.06770405989, 0.1570721263, 0.1434280287, 0.04295191184, -0.07879962265, -0.1610074452, -0.1820744199, -0.1564850599, -0.1117106857, -0.06911197019, -0.03803899989, -0.018976138, -0.008700246907, -0.003698004317, -0.001443221181, -0.0004421770918),
    (-0.06672308627, -0.1353009509, -0.07559650806, 0.05145652305, 0.1328476776, 0.1110923906, 0.01620622731, -0.08318512773, -0.1393111579, -0.1451173835, -0.1191406959, -0.08344766078, -0.05189716398, -0.02921471538, -0.01463357191, -0.005358686102),
    (-0.06188570509, -0.1120544487, -0.03164468805, 0.08318098917, 0.1076065769, 0.02554639647, -0.07633334629, -0.1130798134, -0.07076087078, 0.008202589998, 0.07547632887, 0.1077871043, 0.1068753005, 0.08546497618, 0.0555295236, 0.02380489812),
    (0.07294621453, 0.1170272587, 0.0005822684711, -0.1151664239, -0.08239886349, 0.04808258285, 0.1205972232, 0.06802484515, -0.04264531193, -0.1109041826, -0.09690224579, -0.0289313287, 0.0417153054, 0.07952536804, 0.07530043037, 0.03856509779),
    (0.08652145766, 0.1159240548, -0.04433348034, -0.1318825677, -0.0146605442, 0.1210590442, 0.0842447592, -0.05956973628, -0.1239316034, -0.0494564638, 0.06563154857, 0.1089604688, 0.06071412772, -0.01917666675, -0.06207287706, -0.04244003862),
    (0.09796928773, 0.1014768063, -0.091850156, -0.1080980874, 0.07605361357, 0.1198048209, -0.04229231028, -0.1286411677, -0.01461539232, 0.1112662457, 0.07892093947, -0.04457606115, -0.09810478366, -0.03937820657, 0.03879814661, 0.04335854939),
    (0.1083285032, 0.07708721735, -0.1285703026, -0.0450395491, 0.1354076647, 0.02413735124, -0.1328629117, -0.02187888439, 0.1235455303, 0.03873152733, -0.1025408614, -0.0647085451, 0.06221363399, 0.07559191195, -0.01210690766, -0.04280157103),
    (0.1177268554, 0.04504968521, -0.1441555522, 0.03839419971, 0.1212170689, -0.09675550887, -0.07572314606, 0.120135559, 0.03631601591, -0.1190390193, -0.01579049946, 0.1052262271, 0.01219152635, -0.08172301286, -0.01423910674, 0.04104943366),
    (0.126120285, 0.007979130802, -0.1328480522, 0.1116338241, 0.03421605314, -0.1374354291, 0.07279981158, 0.07996744654, -0.1205095327, -0.004441967651, 0.111290914, -0.04516234118, -0.07618300914, 0.05955705328, 0.03710370067, -0.03825468552),
)
EVEN_GAIN = (
    0.7236012542, -0.7236000597, 0.7230899637, -0.6794753044, 0.309908605, -0.04203461377, 0.003110230195, -0.0001597812355, 6.121678833e-06, -1.82449892e-07,
)
ODD_GAIN = (
    0.7236012257, -0.7235710907, 0.7176666509, -0.5402161025, 0.127514432, -0.01205222733, 0.0007337517912, -3.234542573e-05, 1.088270167e-06, -2.894614862e-08,
)
RANK = 10
TURN = 1.0 / (2.0 * math.pi)
SIN_COEFS = (
    6.283182818550517, -41.3414213986335, 81.59618387150637,
    -76.58010050946145, 41.20539479011024, -12.271262230884131,
)
COS_COEFS = (
    0.9999999891722597, -19.739204532088525, 64.93911898360994, -85.45016554540021,
    60.167831693053074, -25.96831316496443, 6.52961023180932,
)
MODE_TILE = 512
OWN_CLASSES = 4
HALO_CLASSES = 8
NT = (((1,), (1,)), ((), ()))
NN = (((1,), (0,)), ((), ()))
BLOCK_AXES = ("x", "z_hi", "y")
MIB = 1024 * 1024


def horner(coefs, square):
    total = jnp.full_like(square, coefs[-1])
    for coef in coefs[-2::-1]:
        total = total * square + coef
    return total


def cos_sin(turns):
    rest = turns - jnp.round(turns)
    square = rest * rest
    return horner(COS_COEFS, square), rest * horner(SIN_COEFS, square)


def dot(a, b, dims=NN):
    return lax.dot_general(a, b, dims, preferred_element_type=jnp.float32)


def split(value):
    high = value.astype(jnp.bfloat16)
    return high, (value - high.astype(jnp.float32)).astype(jnp.bfloat16)


def split3(value):
    high = value.astype(jnp.bfloat16)
    rest = value - high.astype(jnp.float32)
    middle = rest.astype(jnp.bfloat16)
    return high, middle, (rest - middle.astype(jnp.float32)).astype(jnp.bfloat16)


def dot_split(a, b, dims=NN):
    return dot(a[0], b[0], dims) + (dot(a[0], b[1], dims) + dot(a[1], b[0], dims))


def mixing_matrices():
    parts = []
    for matrix, gain in ((EVEN, None), (ODD, None), (EVEN, EVEN_GAIN), (ODD, ODD_GAIN)):
        matrix = np.array(matrix)
        if gain is not None:
            matrix = matrix / np.array(gain)[:, None]
        rest = np.pad(matrix, ((0, 16 - RANK), (0, 0))).astype(np.float32)
        pieces = []
        for _ in range(3):
            pieces.append(rest.astype(jnp.bfloat16))
            rest = rest - pieces[-1].astype(np.float32)
        first, second, third = pieces
        row = np.concatenate([first, first, second, second, first, third], axis=1)
        parts.append(np.pad(row, ((0, 0), (0, 128 - row.shape[1]))))
    return np.concatenate(parts, axis=1).astype(np.float32)


def mix(matrix, value):
    high, middle, low = split3(value)
    return dot(matrix, jnp.concatenate([high, middle, high, middle, low, high], axis=0))


def factors(first, second, mixing):
    width = first.shape[1]
    index = lax.broadcasted_iota(jnp.int32, (16, 1), 0)
    nodes = jnp.zeros((16, 1), jnp.float32)
    for i, node in enumerate(NODES):
        nodes = jnp.where(index == i, node, nodes)
    cos_part, sin_part = cos_sin(nodes * jnp.concatenate([first, second], axis=1))
    evens = mix(mixing[:, :96], cos_part)
    odds = mix(mixing[:, 128:224], sin_part)
    return evens[:, :width], odds[:, :width], evens[:, width:], odds[:, width:]


def outer_rows(left, right):
    for i in range(0, RANK, 2):
        yield jnp.concatenate([left[:8] * right[i : i + 1], left[:8] * right[i + 1 : i + 2]], axis=0)
    for i in range(8, RANK, 2):
        yield jnp.concatenate([left[i : i + 1] * right[:8], left[i + 1 : i + 2] * right[:8]], axis=0)


PAIR_ROWS = 8 * RANK + 8 * (RANK - 8)


def store_rows(high, low, columns, evx, odx, evy, ody, is_cos, sign):
    pairs = ((evx, evy, 1.0), (odx, ody, sign)) if is_cos else ((odx, evy, 1.0), (evx, ody, 1.0))
    row = 0
    for left, right, factor in pairs:
        if factor < 0:
            right = -right
        for value in outer_rows(left, right):
            part = split(value)
            high[row : row + 16, columns] = part[0]
            low[row : row + 16, columns] = part[1]
            row += 16


def as_column(row):
    count = row.shape[1]
    here = lax.broadcasted_iota(jnp.int32, (count, count), 0)
    there = lax.broadcasted_iota(jnp.int32, (count, count), 1)
    return jnp.sum(jnp.where(here == there, row, 0.0), axis=1, keepdims=True)


def structure_kernel(
    sizes, density_far, packed,
    density, partial, cos_out, sin_out, wave_c_high, wave_c_low, wave_s_high, wave_s_low,
    point_c_high, point_c_low, point_s_high, point_s_low,
    form_c, form_s, arrived,
):
    copy = pltpu.make_async_copy(density_far, density, arrived)
    copy.start()
    views, start = [], 0
    for size in sizes:
        padded = -(-size // 128) * 128
        views.append(packed.at[:, start : start + padded])
        start += padded
    waves, points, centers, mixing = views
    mixing = mixing[...].astype(jnp.bfloat16)
    every = slice(None)
    scale = 2.0 * BAND * TURN
    parts = factors(points[0:1, :] * scale, points[1:2, :] * scale, mixing[:, :256])
    store_rows(point_c_high, point_c_low, every, *parts, True, -1.0)
    store_rows(point_s_high, point_s_low, every, *parts, False, 1.0)
    copy.wait()
    dens = density[...]
    held_c = split(dot(dens, point_c_high[...], NT) + dot(dens, point_c_low[...], NT))
    held_s = split(dot(dens, point_s_high[...], NT) + dot(dens, point_s_low[...], NT))
    center_x = as_column(centers[0:1, :][:, : density.shape[0]])
    center_y = as_column(centers[1:2, :][:, : density.shape[0]])
    atoms, modes = cos_out.shape
    tile = min(MODE_TILE, modes)
    for start in range(0, modes, tile):
        here = slice(start, start + tile)
        kx = waves[0:1, here] * TURN
        ky = waves[1:2, here] * TURN
        parts = factors(kx * (BAND / 24.0), ky * (BAND / 24.0), mixing[:, 256:])
        store_rows(wave_c_high, wave_c_low, here, *parts, True, 1.0)
        store_rows(wave_s_high, wave_s_low, here, *parts, False, 1.0)
        form_c[:, here] = dot_split(held_c, (wave_c_high[:, here], wave_c_low[:, here]))
        form_s[:, here] = dot_split(held_s, (wave_s_high[:, here], wave_s_low[:, here]))
        real = jnp.zeros((16, tile), jnp.float32)
        imag = jnp.zeros((16, tile), jnp.float32)
        for row in range(0, atoms, 16):
            rows = slice(row, row + 16)
            cos_c, sin_c = cos_sin(center_x[rows] * kx + center_y[rows] * ky)
            cos_out[rows, here] = cos_c
            sin_out[rows, here] = sin_c
            cos_f, sin_f = form_c[rows, here], form_s[rows, here]
            real = real + (cos_c * cos_f - sin_c * sin_f)
            imag = imag + (sin_c * cos_f + cos_c * sin_f)
        partial[0:1, here] = jnp.sum(real, axis=0, keepdims=True)
        partial[1:2, here] = -jnp.sum(imag, axis=0, keepdims=True)


def partial_structure(density, centers, points, waves):
    atoms, count = density.shape
    modes = waves.shape[1]
    rows = 2 * PAIR_ROWS
    bf16, f32 = jnp.bfloat16, jnp.float32
    mixing = mixing_matrices()
    parts = [waves, points, centers, mixing]
    sizes = [part.shape[1] for part in parts]
    packed = jnp.concatenate(
        [jnp.pad(p, ((0, 16 - p.shape[0]), (0, -p.shape[1] % 128))) for p in parts], axis=1
    )
    out = lambda shape, kind: jax.ShapeDtypeStruct(shape, kind)
    return pl.pallas_call(
        functools.partial(structure_kernel, sizes),
        in_specs=[pl.BlockSpec(memory_space=pltpu.HBM), pl.BlockSpec(memory_space=pltpu.VMEM)],
        out_shape=[out((atoms, count), bf16), out((2, modes), f32)] + [out((atoms, modes), f32)] * 2
        + [out((rows, modes), bf16)] * 4 + [out((rows, count), bf16)] * 4,
        scratch_shapes=[pltpu.VMEM((atoms, modes), f32)] * 2 + [pltpu.SemaphoreType.DMA],
        compiler_params=pltpu.CompilerParams(vmem_limit_bytes=30 * MIB),
        cost_estimate=pl.CostEstimate(
            flops=16 * atoms * rows * (count * 4 + modes * 6),
            bytes_accessed=8 * atoms * modes, transcendentals=0,
        ),
    )(density, packed)


def far_kernel(
    normalizer, first, second, weight, cos_c, sin_c,
    wave_c_high, wave_c_low, wave_s_high, wave_s_low,
    point_c_high, point_c_low, point_s_high, point_s_low,
    keep, send, spread_c_high, spread_c_low, spread_s_high, spread_s_low, field,
):
    atoms, modes = cos_c.shape
    tile = min(MODE_TILE, modes)
    held_c = held_s = None
    for start in range(0, modes, tile):
        here = slice(start, start + tile)
        scaled = weight[:, here] * normalizer
        real = (first[0:1, here] + second[0:1, here]) * scaled
        imag = (first[1:2, here] + second[1:2, here]) * scaled
        for row in range(0, atoms, 16):
            rows = slice(row, row + 16)
            cosine, sine = cos_c[rows, here], sin_c[rows, here]
            spread_c_high[rows, here], spread_c_low[rows, here] = split(real * cosine - imag * sine)
            spread_s_high[rows, here], spread_s_low[rows, here] = split(-(real * sine + imag * cosine))
        part_c = dot_split(
            (spread_c_high[:, here], spread_c_low[:, here]),
            (wave_c_high[:, here], wave_c_low[:, here]), NT,
        )
        part_s = dot_split(
            (spread_s_high[:, here], spread_s_low[:, here]),
            (wave_s_high[:, here], wave_s_low[:, here]), NT,
        )
        held_c = part_c if held_c is None else held_c + part_c
        held_s = part_s if held_s is None else held_s + part_s
    field[...] = dot_split(
        split(held_c), (point_c_high[...], point_c_low[...])
    ) + dot_split(split(held_s), (point_s_high[...], point_s_low[...]))
    chip, core = lax.axis_index("z_lo"), lax.axis_index("core")
    chips, _, width = keep.shape
    for ahead in range(chips):
        other = jnp.bitwise_xor(chip, ahead)
        mine = pl.multiple_of((2 * other + core) * width, width)
        theirs = pl.multiple_of((2 * other + 1 - core) * width, width)
        keep[ahead] = field[:, pl.ds(mine, width)]
        send[ahead] = field[:, pl.ds(theirs, width)]


def far_partial(normalizer, first, second, weight, cos_c, sin_c, waves, points, chips):
    atoms, modes = cos_c.shape
    rows, count = points[0].shape
    width = count // (2 * chips)
    return pl.pallas_call(
        functools.partial(far_kernel, normalizer),
        out_shape=[jax.ShapeDtypeStruct((chips, atoms, width), jnp.float32)] * 2,
        scratch_shapes=[pltpu.VMEM((atoms, modes), jnp.bfloat16)] * 4
        + [pltpu.VMEM((atoms, count), jnp.float32)],
        compiler_params=pltpu.CompilerParams(vmem_limit_bytes=30 * MIB),
        cost_estimate=pl.CostEstimate(
            flops=2 * atoms * rows * 6 * (count + modes),
            bytes_accessed=8 * atoms * modes, transcendentals=0,
        ),
    )(first, second, weight, cos_c, sin_c, *waves, *points)


def find_places(offsets, atoms_of, counts, atoms):
    classes = offsets.shape[0]
    blocks = lax.axis_size(BLOCK_AXES)
    shift = atoms_of[...] - (lax.axis_index(BLOCK_AXES) - 1) * atoms
    shift = jnp.where(shift < 0, shift + blocks * atoms, shift)
    shift = jnp.where(shift >= blocks * atoms, shift - blocks * atoms, shift)
    live = lax.broadcasted_iota(jnp.int32, shift.shape, 0) < counts[...]
    places = jnp.where(live, shift + 1, 0).astype(jnp.float32)
    of_slot = offsets[...]
    rows = [
        jnp.sum(jnp.where(of_slot == one, places, 0.0), axis=0, keepdims=True)
        for one in range(classes)
    ]
    rows.append(jnp.zeros((-classes % 8, atoms), jnp.float32))
    return jnp.transpose(jnp.concatenate(rows, axis=0))


def near_kernel(group, is_halo, *rest):
    rest, (sources, values, picks, made) = rest[:-4], rest[-4:]
    if is_halo:
        (found, near, start), given, out = rest[:3], rest[3:-1], rest[-1]
    else:
        (offsets, atoms_of, counts, near), given = rest[:4], rest[4:-2]
        out, found = rest[-2:]
        found[...] = find_places(offsets, atoms_of, counts, out.shape[0])
    classes, width, count = near.shape
    atoms = out.shape[0]
    used = atoms * len(given)
    wide = picks.shape[2] // group
    for i, block in enumerate(given):
        sources[i * atoms : (i + 1) * atoms, :] = block[...]
    core = lax.axis_index("core")
    column = lax.broadcasted_iota(jnp.int32, (1, wide), 1)
    if is_halo:
        base = jnp.where(column < atoms, core * 2 * atoms, (1 - core) * 2 * atoms - atoms)
    else:
        base = atoms
    target = jnp.where(column < used, column + base + 1, -1).astype(jnp.float32)
    for slot in range(2):
        for one in range(group):
            values[slot, one * wide + used : (one + 1) * wide, :] = jnp.zeros(
                (wide - used, 2 * width), values.dtype
            )
    result = jnp.zeros((atoms, 2 * width), jnp.float32)
    steps = -(-classes // group)
    for step in range(steps + 1):
        slot = step % 2
        size = min(group, classes - step * group)
        before = group if step < steps else classes - (steps - 1) * group
        if step < steps:
            block = near[step * group : step * group + size].reshape(size * width, count)
            made[slot, :, : size * width] = dot(sources[...], block, NT)
            for one in range(size):
                own_class = step * group + one
                chosen = jnp.where(found[:, own_class : own_class + 1] == target, 1.0, 0.0)
                picks[slot, :, one * wide : (one + 1) * wide] = chosen.astype(jnp.bfloat16)
        if step > 0:
            result = result + dot(
                picks[1 - slot, :, : before * wide], values[1 - slot, : before * wide]
            )
        if step < steps:
            for one in range(size):
                high, low = split(made[slot, :, one * width : (one + 1) * width])
                rows = slice(one * wide, one * wide + used)
                values[slot, rows, :width] = high
                values[slot, rows, width:] = low
    if is_halo:
        begin = start[...]
    else:
        member = lax.axis_index("z_lo") * 2 + core
        mine = pl.multiple_of(member * width, width)
        begin = 0.5 * given[0][:, pl.ds(mine, width)].astype(jnp.float32)
    out[...] = begin + (result[:, :width] + result[:, width:])


def near_part(is_halo, lists, near, start, given):
    atoms = given[0].shape[0]
    classes, width, count = near.shape
    group = min(HALO_CLASSES if is_halo else OWN_CLASSES, classes)
    used = atoms * len(given)
    wide = -(-used // 128) * 128
    bf16, f32 = jnp.bfloat16, jnp.float32
    out = jax.ShapeDtypeStruct((atoms, width), f32)
    found = jax.ShapeDtypeStruct((atoms, -(-classes // 8) * 8), f32)
    return pl.pallas_call(
        functools.partial(near_kernel, group, is_halo),
        scratch_shapes=[
            pltpu.VMEM((used, count), bf16), pltpu.VMEM((2, group * wide, 2 * width), bf16),
            pltpu.VMEM((2, atoms, group * wide), bf16), pltpu.VMEM((2, used, group * width), f32),
        ],
        out_shape=out if is_halo else [out, found],
        compiler_params=pltpu.CompilerParams(vmem_limit_bytes=30 * MIB),
        cost_estimate=pl.CostEstimate(
            flops=2 * used * classes * width * (count + 2 * atoms),
            bytes_accessed=2 * classes * width * count, transcendentals=0,
        ),
    )(*lists, near, *start, *given)


def fold_kernel(keep, taken, *outs):
    for ahead, out in enumerate(outs):
        out[...] = keep[ahead] + taken[ahead]


def fold(keep, taken):
    chips, atoms, width = keep.shape
    return pl.pallas_call(
        fold_kernel,
        out_shape=[jax.ShapeDtypeStruct((atoms, width), jnp.float32)] * chips,
        compiler_params=pltpu.CompilerParams(vmem_limit_bytes=8 * MIB),
    )(keep, taken)


def shifted(value, axis, by):
    count = lax.axis_size(axis)
    return lax.ppermute(value, axis, [(i, (i + by) % count) for i in range(count)])


def sum_over(value, axis):
    count = lax.axis_size(axis)
    return value + sum(shifted(value, axis, by) for by in range(1, count))


def shards(
    density, near_blocks, neighbour_atoms, neighbour_offsets, neighbour_counts,
    centers, local_points, wavevectors, spectral_weight,
):
    atoms, points = density.shape
    blocks = lax.axis_size(BLOCK_AXES)
    modes = wavevectors.shape[1]
    chips, cores = lax.axis_size("z_lo"), lax.axis_size("core")
    normalizer = 1.0 / math.sqrt(atoms * blocks * points * modes * chips * cores)

    halo_route = []
    ring = lax.axis_size("y")
    for source in range(blocks):
        for chip in range(chips):
            for core, target in ((0, (source + 1) % blocks), (1, (source - 1) % blocks)):
                to = chip if source // ring == target // ring else (chip + chips // 2) % chips
                halo_route.append(((source * chips + chip) * 2 + core, (target * chips + to) * 2 + core))
    halo = lax.ppermute(density, BLOCK_AXES + ("z_lo", "core"), halo_route)

    own, partial, cos_c, sin_c, *tables = partial_structure(density, centers, local_points, wavevectors)

    lists = (neighbour_offsets.T, neighbour_atoms.T, neighbour_counts[None, :])
    near_own, found = near_part(False, lists, near_blocks, [], [own])

    structure = sum_over(partial, "x")
    structure = sum_over(structure, "y")
    other_half = shifted(structure, "z_hi", 1)
    halo_other = lax.ppermute(halo, "core", [(0, 1), (1, 0)])

    structure, near_own = lax.optimization_barrier((structure, near_own))
    keep, send = far_partial(
        normalizer, structure, other_half, spectral_weight[None, :], cos_c, sin_c,
        tables[:4], tables[4:], chips,
    )
    taken = lax.ppermute(send, "core", [(0, 1), (1, 0)])
    near_field = near_part(True, [found], near_blocks, [near_own], [halo, halo_other])
    far_field = keep[0] + taken[0]
    for by in range(chips - 1, 0, -1):
        swap = [(i, i ^ by) for i in range(chips)]
        piece = ((keep[by] + taken[by]) * (1.0 / 32.0)).astype(jnp.float16)
        far_field = far_field + lax.ppermute(piece, "z_lo", swap).astype(jnp.float32) * 32.0
    return near_field + far_field


def solution(mesh):
    fine = Mesh(
        mesh.devices.reshape(4, 2, 4, 4, 2), ("x", "z_hi", "y", "z_lo", "core")
    )
    modes = ("z_lo", "core")
    placed = (
        P(BLOCK_AXES, None), P(None, modes, None), P(BLOCK_AXES, None), P(BLOCK_AXES, None),
        P(BLOCK_AXES), P(None, BLOCK_AXES), P(), P(None, modes), P(modes),
    )
    return jax.shard_map(
        shards, mesh=fine, in_specs=placed, out_specs=P(BLOCK_AXES, modes), check_vma=False
    )
```
